32 devices in a mesh: grp: 2 (over x), head: 16 (over z, y, core).
Axes of the slice: x: 2, y: 2, z: 4, core: 2. Of those that a mesh axis runs over, the one named last changes fastest.
Arguments:
- tokens: bfloat16 [256, 16384], P('grp', 'head'), parts along dimension 0, may hold values from -14 to 14
- positions: int32 [256], P('grp'), parts along dimension 0, may hold values from 0 to 127, each once
- q_weight: bfloat16 [16384, 2048], P(None, 'head'), may hold values from -0.046875 to 0.046875
- kv_weight: bfloat16 [16384, 256], P('head'), may hold values from -0.046875 to 0.046875
- o_weight: bfloat16 [2048, 16384], P('head'), may hold values from -0.125 to 0.125
Outputs:
- attended: bfloat16 [256, 16384], P('grp', 'head'), parts along dimension 0
The draws below stay inside these ranges and needn't reach their ends.
There are 2 independent parts, one for each index of `grp`. The reference program is written for one: setup_inputs(seed, part) draws one part's arguments, and reference() takes and returns one part's arrays. A program takes and returns all parts, laid end to end along the dimension named above; an argument that names none is the same for every part. Nothing has to cross between parts.
Inputs may be any that keep to these rules, and one draw needn't show every extreme that they name: `positions`: each of 0 to 127 appears exactly once.
All inputs are finite; a program needn't handle non-finite values.
Results may differ from the reference program's by a relative error of at most 0.012.
The reference program's roundings to bfloat16 on the way (of `weights` and `context`) count: a program that leaves them out, or rounds other values in their place, can miss the bound.
Values may be sent and summed in bfloat16 or wider, within the bound.
A program may use at most 64 MiB of HBM per device.

```python
import jax
import jax.numpy as jnp
from jax import lax

D = 16384
HD = 128
GROUP = 16
TOKENS = 128
HEADS = 16
KV_HEADS = 1


def draw_tokens(key, part):
    key = jax.random.fold_in(key, 7)
    base = jax.random.normal(jax.random.fold_in(key, 3), (TOKENS, D), jnp.float32)
    return jnp.clip(base, -6.0, 6.0).astype(jnp.bfloat16)


def steps_of(stream_key, extent, cuts, smallest, largest):
    loudness = 1.0
    for position, blocks in cuts:
        steps = jax.random.uniform(jax.random.fold_in(jax.random.fold_in(stream_key, 6), position), (blocks,), jnp.float32, smallest / len(cuts), largest / len(cuts))
        loudness = loudness * jnp.repeat(jnp.exp(steps), extent[position] // blocks).reshape((-1,) + (1,) * (len(extent) - 1 - position))
    return loudness


def noise(stream_key, shape, spread, bound, shards=(), kind=jnp.bfloat16):
    loudness = steps_of(stream_key, shape, shards, -0.22, 0.18) if shards else 1.0
    array = jax.random.normal(stream_key, shape, jnp.float32) * spread * loudness
    return jnp.minimum(jnp.maximum(array, -bound), bound).astype(kind)


def setup_inputs(seed: int = 0, part: int = 0) -> dict:
    splits = jax.random.split(jax.random.key(seed), 6)
    own_keys = jax.random.split(jax.random.fold_in(splits[5], part), 6)
    tokens = draw_tokens(jax.random.fold_in(jax.random.fold_in(splits[5], part), 71), part)
    positions = jax.random.permutation(own_keys[1], TOKENS).astype(jnp.int32)
    q_weight = noise(splits[2], (D, HEADS * HD), D ** -0.5, 0.046875, ((1, 16),))
    kv_weight = noise(splits[3], (D, 2 * KV_HEADS * HD), D ** -0.5, 0.046875, ((0, 16),))
    o_weight = noise(splits[4], (HEADS * HD, D), (HEADS * HD) ** -0.5, 0.125, ((0, 16),))
    return dict(tokens=tokens, positions=positions, q_weight=q_weight, kv_weight=kv_weight, o_weight=o_weight)


def rotate(vals, positions):
    half = vals.shape[-1] // 2
    inverse = 500000.0 ** (-(jnp.arange(half, dtype=jnp.float32) * 2.0 / vals.shape[-1]))
    angles = positions.astype(jnp.float32)[:, None] * inverse[None, :]
    cosine = jnp.cos(angles)[:, None, :]
    sine = jnp.sin(angles)[:, None, :]
    first = vals[..., :half]
    second = vals[..., half:]
    return jnp.concatenate([first * cosine - second * sine, second * cosine + first * sine], axis=-1)

def reference(tokens, positions, q_weight, kv_weight, o_weight):
    q_raw = jnp.dot(tokens, q_weight, preferred_element_type=jnp.float32).reshape(TOKENS, HEADS, HD)
    kv_raw = jnp.dot(tokens, kv_weight, preferred_element_type=jnp.float32)
    k_raw = kv_raw[:, :KV_HEADS * HD].reshape(TOKENS, KV_HEADS, HD)
    values = kv_raw[:, KV_HEADS * HD:].reshape(TOKENS, KV_HEADS, HD).astype(jnp.bfloat16)
    queries = rotate(q_raw, positions).astype(jnp.bfloat16)
    keys = rotate(k_raw, positions).astype(jnp.bfloat16)
    keys_all = jnp.repeat(keys, GROUP, axis=1).astype(jnp.float32)
    values_all = jnp.repeat(values, GROUP, axis=1).astype(jnp.float32)
    scores = jnp.einsum('qhd,khd->hqk', queries.astype(jnp.float32), keys_all) / jnp.sqrt(jnp.float32(HD))
    allowed = positions[None, :] <= positions[:, None]
    scores = jnp.where(allowed[None], scores, -1e+30)
    peak = lax.optimization_barrier(jnp.max(scores, axis=-1, keepdims=True))
    expo = jnp.where(allowed[None], jnp.exp(scores - peak), 0.0)
    weights = (expo / lax.optimization_barrier(jnp.sum(expo, axis=-1, keepdims=True))).astype(jnp.bfloat16)
    context = jnp.einsum('hqk,khd->qhd', weights.astype(jnp.float32), values_all)
    context = context.astype(jnp.bfloat16).reshape(TOKENS, HEADS * HD)
    return jnp.dot(context, o_weight, preferred_element_type=jnp.float32).astype(jnp.bfloat16)
```

```python
import functools

import jax
import jax.numpy as jnp
from jax import lax
from jax.experimental import pallas as pl
from jax.experimental.pallas import tpu as pltpu
from jax.sharding import PartitionSpec as P

HD = 128
GROUP = 16


def rotate(vals, positions):
    half = vals.shape[-1] // 2
    inverse = 500000.0 ** (-(jnp.arange(half, dtype=jnp.float32) * 2.0 / vals.shape[-1]))
    angles = positions.astype(jnp.float32)[:, None] * inverse[None, :]
    cosine = jnp.cos(angles)[:, None, :]
    sine = jnp.sin(angles)[:, None, :]
    first = vals[..., :half]
    second = vals[..., half:]
    return jnp.concatenate(
        [first * cosine - second * sine, second * cosine + first * sine], axis=-1
    )


def on_device(tokens, positions, q_weight, kv_weight, o_weight):
    count_tok = tokens.shape[0]
    width = q_weight.shape[1]
    head_size = HD
    local_heads = width // head_size
    kv_width = kv_weight.shape[1]
    kv_half = kv_width // 2
    first_head = lax.axis_index("head") * local_heads
    kv_index = first_head // GROUP
    q_raw = jnp.dot(
        lax.all_gather(tokens, "head", axis=1, tiled=True),
        q_weight,
        preferred_element_type=jnp.float32,
    )
    partial_value = jnp.dot(tokens, kv_weight, preferred_element_type=jnp.float32)
    kv_raw = lax.psum(partial_value, "head")
    k_raw = lax.dynamic_slice_in_dim(kv_raw, kv_index * head_size, head_size, 1)
    v_raw = lax.dynamic_slice_in_dim(kv_raw, kv_half + kv_index * head_size, head_size, 1)
    queries = rotate(q_raw.reshape(count_tok, local_heads, head_size), positions).astype(
        jnp.bfloat16
    )
    keys = rotate(k_raw.reshape(count_tok, 1, head_size), positions)[:, 0, :].astype(jnp.bfloat16)
    values = v_raw.astype(jnp.bfloat16)
    scores = jnp.einsum(
        "qhd,kd->hqk", queries, keys, preferred_element_type=jnp.float32
    ) / jnp.sqrt(jnp.float32(head_size))
    allowed = positions[None, :] <= positions[:, None]
    scores = jnp.where(allowed[None], scores, -1e30)
    peak = jnp.max(scores, axis=-1, keepdims=True)
    expo = jnp.where(allowed[None], jnp.exp(scores - peak), 0.0)
    weights = (expo / jnp.sum(expo, axis=-1, keepdims=True)).astype(jnp.bfloat16)
    context = jnp.einsum("hqk,kd->qhd", weights, values, preferred_element_type=jnp.float32)
    context = context.astype(jnp.bfloat16).reshape(count_tok, width)
    summed = lax.psum_scatter(
        lax.dot_general(
            o_weight, context, (((0,), (1,)), ((), ())), preferred_element_type=jnp.float32
        ),
        "head",
        scatter_dimension=0,
        tiled=True,
    ).T
    return summed.astype(jnp.bfloat16)


RING = 8
CORES = 2


def head_at(place, core):
    side = lax.div(place, RING // 2)
    level = place * (1 - side) + (RING - 1 - place) * side
    return (level * 2 + side) * CORES + core


def fused(
    cos_ref, sin_ref, pos_col, pos_row, tok_hbm, q_hbm, kv_hbm, o_hbm, out_ref,
    tok, qw, kvw, ow, q_acc, q_send, q_recv, kv_part, kv_sib, kv_sum, kv_in, kv_all,
    ctx, part, rs_send, rs_recv,
    tok_sem, kvw_sem, q_sem, q_out, q_in, o_sem, o_out, o_in,
    ag_out, ag_in, pair_out, pair_in, kr_out, kr_in, ka_out, ka_in, rs_out, rs_in,
):
    rows, width = out_ref.shape
    half_w = width // 2
    half_r = rows // 2
    piece = rows // RING
    me = lax.axis_index("head")
    core = lax.rem(me, CORES)
    chip = lax.div(me, CORES)
    side = lax.rem(chip, 2)
    level = lax.div(chip, 2)
    place = level * (1 - side) + (RING - 1 - level) * side

    def at(offset, which):
        return head_at(lax.rem(place + offset + RING, RING), which)

    sibling = chip * CORES + (1 - core)
    right = at(1, core)
    left = at(-1, core)

    def push(src, dst, send, recv, target):
        copy = pltpu.make_async_remote_copy(
            src_ref=src, dst_ref=dst, send_sem=send, recv_sem=recv,
            device_id={"head": target}, device_id_type=pl.DeviceIdType.MESH,
        )
        copy.start()
        return copy

    def pull(src, dst, sem):
        copy = pltpu.make_async_copy(src, dst, sem)
        copy.start()
        return copy

    sent = []
    tok_local = [
        pull(tok_hbm.at[:, pl.ds(b * half_w, half_w)], tok.at[0, b], tok_sem.at[b])
        for b in range(2)
    ]
    kvw_local = pull(kv_hbm, kvw, kvw_sem)

    barrier = pltpu.get_barrier_semaphore()
    for offset in range(RING):
        for other in range(CORES):
            if offset or other:
                pl.semaphore_signal(
                    barrier, inc=1,
                    device_id={"head": at(offset, lax.rem(core + other, CORES))},
                    device_id_type=pl.DeviceIdType.MESH,
                )
    pl.semaphore_wait(barrier, RING * CORES - 1)

    ways = (right, left)

    def shard(way, hop):
        return hop if way == 0 else (RING - hop) % RING

    def ag_send(i):
        for way in range(2):
            b = (i + way) % 2
            hop = i // 2
            if hop == 0:
                source = tok_hbm.at[:, pl.ds(b * half_w, half_w)]
            else:
                source = tok.at[shard(way, hop), b]
            sent.append(push(
                source, tok.at[shard(way, hop + 1), b],
                ag_out.at[way, i], ag_in.at[way, i], ways[way],
            ))

    def ag_wait(i, way):
        b = (i + way) % 2
        slot = tok.at[shard(way, i // 2 + 1), b]
        pltpu.make_async_remote_copy(
            src_ref=slot, dst_ref=slot, send_sem=ag_out.at[way, i], recv_sem=ag_in.at[way, i],
            device_id={"head": ways[1 - way]}, device_id_type=pl.DeviceIdType.MESH,
        ).wait_recv()

    def q_add(slot, b):
        q_acc[...] += jnp.dot(
            tok[slot, b], qw[slot, b * half_w:(b + 1) * half_w, :],
            preferred_element_type=jnp.float32,
        )

    last = 2 * (RING // 2 - 1)
    ag_send(0)
    ag_send(1)

    q_local, q_pair = [], []
    for r in range(RING):
        owner = lax.div(at(-r, core), CORES)
        q_local.append(pull(q_hbm.at[owner, core], qw.at[r, :, 0:HD], q_sem.at[r]))
        q_pair.append(push(
            q_hbm.at[owner, 1 - core], qw.at[r, :, HD:2 * HD], q_out.at[r], q_in.at[r], sibling
        ))
    sent += q_pair

    for copy in tok_local:
        copy.wait()
    kvw_local.wait()
    both = jnp.dot(tok[0, 0], kvw[0:half_w, :], preferred_element_type=jnp.float32)
    both += jnp.dot(tok[0, 1], kvw[half_w:width, :], preferred_element_type=jnp.float32)
    kv_part[0] = both[:, 0:HD]
    kv_part[1] = both[:, HD:2 * HD]
    kv_pair = push(kv_part.at[1 - core], kv_sib, pair_out.at[0], pair_in.at[0], sibling)
    sent.append(kv_pair)

    def step(i):
        for way in range(2):
            ag_wait(i, way)
        if i + 2 <= last:
            ag_send(i + 2)

    step(0)
    kv_pair.wait_recv()
    kv_sum[...] = (kv_part[core] + kv_sib[...]).reshape(RING, piece, HD)
    kv_rows = []
    for r in range(1, RING):
        to = lax.rem(place + r, RING)
        kv_rows.append(push(
            kv_sum.at[to], kv_in.at[r], kr_out.at[r], kr_in.at[r], at(r, core)
        ))
    sent += kv_rows

    step(1)
    o_local, o_pair = [], []
    for r in range(RING):
        mine = pl.multiple_of(at(-r, core) * width, width)
        theirs = pl.multiple_of(at(-r, 1 - core) * width, width)
        o_local.append(pull(o_hbm.at[:, pl.ds(mine, width)], ow.at[r, 0:HD], o_sem.at[r]))
        o_pair.append(push(
            o_hbm.at[:, pl.ds(theirs, width)], ow.at[r, HD:2 * HD], o_out.at[r], o_in.at[r],
            sibling,
        ))
    sent += o_pair
    q_acc[...] = jnp.zeros_like(q_acc)
    for r in range(RING):
        q_local[r].wait()
        q_pair[r].wait_recv()

    for b in range(2):
        q_add(0, b)
    for i in range(2):
        for way in range(2):
            q_add(shard(way, i // 2 + 1), (i + way) % 2)

    for i in range(2, last + 1):
        step(i)
        if i == 2:
            total = kv_sum[place]
            for r in range(1, RING):
                kv_rows[r - 1].wait_recv()
                total += kv_in[r]
            turned = total * cos_ref[place] + pltpu.roll(total, HD // 2, 1) * sin_ref[place]
            is_key = (core == 0).astype(jnp.float32)
            kv_all[core, place] = (turned * is_key + total * (1.0 - is_key)).astype(jnp.bfloat16)
            kv_out = []
            for r in range(RING):
                for other in range(CORES):
                    if r or other:
                        kv_out.append(push(
                            kv_all.at[core, place], kv_all.at[core, place],
                            ka_out.at[other, r], ka_in.at[other, r],
                            at(r, lax.rem(core + other, CORES)),
                        ))
            sent += kv_out
        for way in range(2):
            q_add(shard(way, i // 2 + 1), (i + way) % 2)

    q_send[...] = q_acc[:, HD:2 * HD]
    q_pass = push(q_send, q_recv, pair_out.at[1], pair_in.at[1], sibling)
    sent.append(q_pass)
    for copy in kv_out:
        copy.wait_recv()
    q_pass.wait_recv()
    q_raw = q_acc[:, 0:HD] + q_recv[...]
    cosine = cos_ref[...].reshape(rows, HD)
    sine = sin_ref[...].reshape(rows, HD)
    queries = (q_raw * cosine + pltpu.roll(q_raw, HD // 2, 1) * sine).astype(jnp.bfloat16)
    keys = kv_all[0].reshape(rows, HD)
    values = kv_all[1].reshape(rows, HD)
    scores = lax.dot_general(
        queries, keys, (((1,), (1,)), ((), ())), preferred_element_type=jnp.float32
    ) * (HD ** -0.5)
    allowed = pos_row[...] <= pos_col[...]
    scores = jnp.where(allowed, scores, -1e30)
    peak = jnp.max(scores, axis=-1, keepdims=True)
    expo = jnp.where(allowed, jnp.exp(scores - peak), 0.0)
    weights = (expo / jnp.sum(expo, axis=-1, keepdims=True)).astype(jnp.bfloat16)
    ctx[0] = jnp.dot(weights, values, preferred_element_type=jnp.float32).astype(jnp.bfloat16)
    ctx_pass = push(ctx.at[0], ctx.at[1], pair_out.at[2], pair_in.at[2], sibling)
    sent.append(ctx_pass)
    for r in range(RING):
        o_local[r].wait()
        o_pair[r].wait_recv()
    ctx_pass.wait_recv()

    context = jnp.concatenate([ctx[0], ctx[1]], axis=1)
    tile = 2 * HD

    def project(slot):
        for n in range(width // tile):
            part[slot, :, n * tile:(n + 1) * tile] = jnp.dot(
                context, ow[slot, :, n * tile:(n + 1) * tile], preferred_element_type=jnp.float32
            )

    def rs_wait(i, way):
        slot = rs_recv.at[way, i]
        pltpu.make_async_remote_copy(
            src_ref=slot, dst_ref=slot, send_sem=rs_out.at[way, i], recv_sem=rs_in.at[way, i],
            device_id={"head": ways[1 - way]}, device_id_type=pl.DeviceIdType.MESH,
        ).wait_recv()

    def rs_go(i):
        hop = (i + 1) // 2
        for way in range(2):
            slot = RING // 2 + hop if way == 0 else RING // 2 - hop
            b = (i + way) % 2
            value = part[slot, b * half_r:(b + 1) * half_r, :]
            if i >= 2:
                rs_wait(i - 2, way)
                value += rs_recv[way, i - 2].astype(jnp.float32)
            rs_send[way, i] = value.astype(jnp.bfloat16)
            sent.append(push(
                rs_send.at[way, i], rs_recv.at[way, i], rs_out.at[way, i], rs_in.at[way, i],
                ways[way],
            ))

    project(RING // 2)
    rs_go(0)
    for hop in range(1, RING // 2):
        project(RING // 2 + hop)
        project(RING // 2 - hop)
        rs_go(2 * hop - 1)
        if hop == RING // 2 - 1:
            project(0)
        rs_go(2 * hop)
    for i in (last - 1, last):
        for way in range(2):
            b = (i + way) % 2
            rs_wait(i, way)
            part[0, b * half_r:(b + 1) * half_r, :] += rs_recv[way, i].astype(jnp.float32)
    out_ref[...] = part[0].astype(out_ref.dtype)
    for copy in sent:
        copy.wait_send()


def on_ring(tokens, positions, q_weight, kv_weight, o_weight):
    rows, width = tokens.shape
    half = HD // 2
    inverse = 500000.0 ** (-(jnp.arange(half, dtype=jnp.float32) * 2.0 / HD))
    angles = positions.astype(jnp.float32)[:, None] * inverse[None, :]
    cosine, sine = jnp.cos(angles), jnp.sin(angles)
    piece = rows // RING
    cosine = jnp.concatenate([cosine, cosine], axis=1).reshape(RING, piece, HD)
    sine = jnp.concatenate([-sine, sine], axis=1).reshape(RING, piece, HD)
    hops = RING - 1
    any_space = pl.BlockSpec(memory_space=pl.ANY)
    vmem = pl.BlockSpec(memory_space=pltpu.VMEM)
    bf16, f32 = jnp.bfloat16, jnp.float32
    dma = pltpu.SemaphoreType.DMA
    return pl.pallas_call(
        fused,
        out_shape=jax.ShapeDtypeStruct((rows, width), bf16),
        in_specs=[vmem] * 4 + [any_space] * 4,
        out_specs=vmem,
        scratch_shapes=[
            pltpu.VMEM((RING, 2, rows, width // 2), bf16),
            pltpu.VMEM((RING, width, 2 * HD), bf16),
            pltpu.VMEM((width, 2 * HD), bf16),
            pltpu.VMEM((RING, 2 * HD, width), bf16),
            pltpu.VMEM((rows, 2 * HD), f32),
            pltpu.VMEM((rows, HD), f32),
            pltpu.VMEM((rows, HD), f32),
            pltpu.VMEM((2, rows, HD), f32),
            pltpu.VMEM((rows, HD), f32),
            pltpu.VMEM((RING, piece, HD), f32),
            pltpu.VMEM((RING, piece, HD), f32),
            pltpu.VMEM((2, RING, piece, HD), bf16),
            pltpu.VMEM((2, rows, HD), bf16),
            pltpu.VMEM((RING, rows, width), f32),
            pltpu.VMEM((2, hops, rows // 2, width), bf16),
            pltpu.VMEM((2, hops, rows // 2, width), bf16),
            dma((2,)), dma, dma((RING,)), dma((RING,)), dma((RING,)),
            dma((RING,)), dma((RING,)), dma((RING,)),
            dma((2, hops)), dma((2, hops)), dma((3,)), dma((3,)),
            dma((RING,)), dma((RING,)), dma((2, RING)), dma((2, RING)),
            dma((2, hops)), dma((2, hops)),
        ],
        compiler_params=pltpu.CompilerParams(
            collective_id=0, has_side_effects=True, vmem_limit_bytes=48 * 2**20
        ),
        name="prefill_ring",
    )(
        cosine, sine, positions[:, None], positions[None, :],
        tokens, q_weight.reshape(RING, CORES, width, HD), kv_weight, o_weight,
    )


def solution(mesh):
    ring = mesh.shape["head"] == RING * CORES
    return jax.shard_map(
        on_ring if ring else on_device,
        mesh=mesh,
        in_specs=(P("grp", "head"), P("grp"), P(None, "head"), P("head", None), P("head", None)),
        out_specs=P("grp", "head"),
        check_vma=False,
    )
```

```python
import math

import jax
import jax.numpy as jnp
from jax import lax
from jax.experimental import pallas as pl
from jax.experimental.pallas import tpu as pltpu
from jax.sharding import PartitionSpec as P

HD = 128
GROUP = 16


def rotate(vals, positions):
    half = vals.shape[-1] // 2
    inverse = 500000.0 ** (-(jnp.arange(half, dtype=jnp.float32) * 2.0 / vals.shape[-1]))
    angles = positions.astype(jnp.float32)[:, None] * inverse[None, :]
    cosine = jnp.cos(angles)[:, None, :]
    sine = jnp.sin(angles)[:, None, :]
    first = vals[..., :half]
    second = vals[..., half:]
    return jnp.concatenate(
        [first * cosine - second * sine, second * cosine + first * sine], axis=-1
    )


def on_device(tokens, positions, q_weight, kv_weight, o_weight):
    count_tok = tokens.shape[0]
    width = q_weight.shape[1]
    head_size = HD
    local_heads = width // head_size
    kv_width = kv_weight.shape[1]
    kv_half = kv_width // 2
    first_head = lax.axis_index("head") * local_heads
    kv_index = first_head // GROUP
    q_raw = jnp.dot(
        lax.all_gather(tokens, "head", axis=1, tiled=True),
        q_weight,
        preferred_element_type=jnp.float32,
    )
    partial_value = jnp.dot(tokens, kv_weight, preferred_element_type=jnp.float32)
    kv_raw = lax.psum(partial_value, "head")
    k_raw = lax.dynamic_slice_in_dim(kv_raw, kv_index * head_size, head_size, 1)
    v_raw = lax.dynamic_slice_in_dim(kv_raw, kv_half + kv_index * head_size, head_size, 1)
    queries = rotate(q_raw.reshape(count_tok, local_heads, head_size), positions).astype(
        jnp.bfloat16
    )
    keys = rotate(k_raw.reshape(count_tok, 1, head_size), positions)[:, 0, :].astype(jnp.bfloat16)
    values = v_raw.astype(jnp.bfloat16)
    scores = jnp.einsum(
        "qhd,kd->hqk", queries, keys, preferred_element_type=jnp.float32
    ) / jnp.sqrt(jnp.float32(head_size))
    allowed = positions[None, :] <= positions[:, None]
    scores = jnp.where(allowed[None], scores, -1e30)
    peak = jnp.max(scores, axis=-1, keepdims=True)
    expo = jnp.where(allowed[None], jnp.exp(scores - peak), 0.0)
    weights = (expo / jnp.sum(expo, axis=-1, keepdims=True)).astype(jnp.bfloat16)
    context = jnp.einsum("hqk,kd->qhd", weights, values, preferred_element_type=jnp.float32)
    context = context.astype(jnp.bfloat16).reshape(count_tok, width)
    summed = lax.psum_scatter(
        lax.dot_general(
            o_weight, context, (((0,), (1,)), ((), ())), preferred_element_type=jnp.float32
        ),
        "head",
        scatter_dimension=0,
        tiled=True,
    ).T
    return summed.astype(jnp.bfloat16)


RING = 8
CORES = 2


def head_at(place, core):
    side = lax.div(place, RING // 2)
    level = place * (1 - side) + (RING - 1 - place) * side
    return (level * 2 + side) * CORES + core


def fused(
    pos_hbm, tok_hbm, q_hbm, kv_hbm, o_hbm, out_ref, pos, cos_ref, sin_ref,
    tok, qw, kvw, ow, q_acc, q_send, q_recv, kv_part, kv_sib, kv_sum, kv_in, kv_all,
    ctx, part, rs_send, rs_recv,
    pos_sem, tok_sem, kvw_sem, q_sem, q_out, q_in, o_sem, o_out, o_in,
    ag_out, ag_in, pair_out, pair_in, kr_out, kr_in, ka_out, ka_in, rs_out, rs_in,
):
    rows, width = out_ref.shape
    half_w = width // 2
    half_r = rows // 2
    piece = rows // RING
    me = lax.axis_index("head")
    core = lax.rem(me, CORES)
    chip = lax.div(me, CORES)
    side = lax.rem(chip, 2)
    level = lax.div(chip, 2)
    place = level * (1 - side) + (RING - 1 - level) * side

    def at(offset, which):
        return head_at(lax.rem(place + offset + RING, RING), which)

    sibling = chip * CORES + (1 - core)
    right = at(1, core)
    left = at(-1, core)

    def push(src, dst, send, recv, target):
        copy = pltpu.make_async_remote_copy(
            src_ref=src, dst_ref=dst, send_sem=send, recv_sem=recv,
            device_id={"head": target}, device_id_type=pl.DeviceIdType.MESH,
        )
        copy.start()
        return copy

    def pull(src, dst, sem):
        copy = pltpu.make_async_copy(src, dst, sem)
        copy.start()
        return copy

    sent = []
    pos_local = pull(pos_hbm, pos, pos_sem)
    tok_local = [
        pull(tok_hbm.at[:, pl.ds(b * half_w, half_w)], tok.at[0, b], tok_sem.at[b])
        for b in range(2)
    ]
    kvw_local = pull(kv_hbm, kvw, kvw_sem)

    barrier = pltpu.get_barrier_semaphore()
    for offset in range(RING):
        for other in range(CORES):
            if offset or other:
                pl.semaphore_signal(
                    barrier, inc=1,
                    device_id={"head": at(offset, lax.rem(core + other, CORES))},
                    device_id_type=pl.DeviceIdType.MESH,
                )
    pl.semaphore_wait(barrier, RING * CORES - 1)

    ways = (right, left)

    def shard(way, hop):
        return hop if way == 0 else (RING - hop) % RING

    def ag_send(i):
        for way in range(2):
            b = (i + way) % 2
            hop = i // 2
            if hop == 0:
                source = tok_hbm.at[:, pl.ds(b * half_w, half_w)]
            else:
                source = tok.at[shard(way, hop), b]
            sent.append(push(
                source, tok.at[shard(way, hop + 1), b],
                ag_out.at[way, i], ag_in.at[way, i], ways[way],
            ))

    def ag_wait(i, way):
        b = (i + way) % 2
        slot = tok.at[shard(way, i // 2 + 1), b]
        pltpu.make_async_remote_copy(
            src_ref=slot, dst_ref=slot, send_sem=ag_out.at[way, i], recv_sem=ag_in.at[way, i],
            device_id={"head": ways[1 - way]}, device_id_type=pl.DeviceIdType.MESH,
        ).wait_recv()

    def q_add(slot, b):
        q_acc[...] += jnp.dot(
            tok[slot, b], qw[slot, b * half_w:(b + 1) * half_w, :],
            preferred_element_type=jnp.float32,
        )

    last = 2 * (RING // 2 - 1)
    ag_send(0)
    ag_send(1)

    q_local, q_pair = [], []
    for r in range(RING):
        owner = lax.div(at(-r, core), CORES)
        q_local.append(pull(q_hbm.at[owner, core], qw.at[r, :, 0:HD], q_sem.at[r]))
        q_pair.append(push(
            q_hbm.at[owner, 1 - core], qw.at[r, :, HD:2 * HD], q_out.at[r], q_in.at[r], sibling
        ))
    sent += q_pair

    pos_local.wait()
    pos_row = jnp.broadcast_to(pos[...].astype(jnp.float32), (rows, rows))
    pos_col = pos_row.T
    allowed = pos_row <= pos_col
    lane = lax.broadcasted_iota(jnp.int32, (rows, HD), 1)
    angle_step = lax.rem(lane, HD // 2).astype(jnp.float32) * (2.0 / HD)
    angles = pos_col * jnp.exp(angle_step * -math.log(500000.0))
    sine = jnp.sin(angles)
    cos_ref[...] = jnp.cos(angles).reshape(RING, piece, HD)
    sin_ref[...] = jnp.where(lane < HD // 2, -sine, sine).reshape(RING, piece, HD)

    for copy in tok_local:
        copy.wait()
    kvw_local.wait()
    both = jnp.dot(tok[0, 0], kvw[0:half_w, :], preferred_element_type=jnp.float32)
    both += jnp.dot(tok[0, 1], kvw[half_w:width, :], preferred_element_type=jnp.float32)
    kv_part[0] = both[:, 0:HD]
    kv_part[1] = both[:, HD:2 * HD]
    kv_pair = push(kv_part.at[1 - core], kv_sib, pair_out.at[0], pair_in.at[0], sibling)
    sent.append(kv_pair)

    def step(i):
        for way in range(2):
            ag_wait(i, way)
        if i + 2 <= last:
            ag_send(i + 2)

    step(0)
    kv_pair.wait_recv()
    kv_sum[...] = (kv_part[core] + kv_sib[...]).reshape(RING, piece, HD)
    kv_rows = []
    for r in range(1, RING):
        to = lax.rem(place + r, RING)
        kv_rows.append(push(
            kv_sum.at[to], kv_in.at[r], kr_out.at[r], kr_in.at[r], at(r, core)
        ))
    sent += kv_rows

    step(1)
    o_local, o_pair = [], []
    for r in range(RING):
        mine = pl.multiple_of(at(-r, core) * width, width)
        theirs = pl.multiple_of(at(-r, 1 - core) * width, width)
        o_local.append(pull(o_hbm.at[:, pl.ds(mine, width)], ow.at[r, 0:HD], o_sem.at[r]))
        o_pair.append(push(
            o_hbm.at[:, pl.ds(theirs, width)], ow.at[r, HD:2 * HD], o_out.at[r], o_in.at[r],
            sibling,
        ))
    sent += o_pair
    q_acc[...] = jnp.zeros_like(q_acc)
    for r in range(RING):
        q_local[r].wait()
        q_pair[r].wait_recv()

    for b in range(2):
        q_add(0, b)
    for i in range(2):
        for way in range(2):
            q_add(shard(way, i // 2 + 1), (i + way) % 2)

    for i in range(2, last + 1):
        step(i)
        if i == 2:
            total = kv_sum[place]
            for r in range(1, RING):
                kv_rows[r - 1].wait_recv()
                total += kv_in[r]
            turned = total * cos_ref[place] + pltpu.roll(total, HD // 2, 1) * sin_ref[place]
            is_key = (core == 0).astype(jnp.float32)
            kv_all[core, place] = (turned * is_key + total * (1.0 - is_key)).astype(jnp.bfloat16)
            kv_out = []
            for r in range(RING):
                for other in range(CORES):
                    if r or other:
                        kv_out.append(push(
                            kv_all.at[core, place], kv_all.at[core, place],
                            ka_out.at[other, r], ka_in.at[other, r],
                            at(r, lax.rem(core + other, CORES)),
                        ))
            sent += kv_out
        for way in range(2):
            q_add(shard(way, i // 2 + 1), (i + way) % 2)

    q_send[...] = q_acc[:, HD:2 * HD]
    q_pass = push(q_send, q_recv, pair_out.at[1], pair_in.at[1], sibling)
    sent.append(q_pass)
    for copy in kv_out:
        copy.wait_recv()
    q_pass.wait_recv()
    q_raw = q_acc[:, 0:HD] + q_recv[...]
    cosine = cos_ref[...].reshape(rows, HD)
    sine = sin_ref[...].reshape(rows, HD)
    queries = (q_raw * cosine + pltpu.roll(q_raw, HD // 2, 1) * sine).astype(jnp.bfloat16)
    keys = kv_all[0].reshape(rows, HD)
    values = kv_all[1].reshape(rows, HD)
    scores = lax.dot_general(
        queries, keys, (((1,), (1,)), ((), ())), preferred_element_type=jnp.float32
    ) * (HD ** -0.5)
    scores = jnp.where(allowed, scores, -1e30)
    peak = jnp.max(scores, axis=-1, keepdims=True)
    expo = jnp.where(allowed, jnp.exp(scores - peak), 0.0)
    weights = (expo / jnp.sum(expo, axis=-1, keepdims=True)).astype(jnp.bfloat16)
    ctx[0] = jnp.dot(weights, values, preferred_element_type=jnp.float32).astype(jnp.bfloat16)
    ctx_pass = push(ctx.at[0], ctx.at[1], pair_out.at[2], pair_in.at[2], sibling)
    sent.append(ctx_pass)
    for r in range(RING):
        o_local[r].wait()
        o_pair[r].wait_recv()
    ctx_pass.wait_recv()

    context = jnp.concatenate([ctx[0], ctx[1]], axis=1)
    tile = 2 * HD

    def project(slot):
        for n in range(width // tile):
            part[slot, :, n * tile:(n + 1) * tile] = jnp.dot(
                context, ow[slot, :, n * tile:(n + 1) * tile], preferred_element_type=jnp.float32
            )

    def rs_wait(i, way):
        slot = rs_recv.at[way, i]
        pltpu.make_async_remote_copy(
            src_ref=slot, dst_ref=slot, send_sem=rs_out.at[way, i], recv_sem=rs_in.at[way, i],
            device_id={"head": ways[1 - way]}, device_id_type=pl.DeviceIdType.MESH,
        ).wait_recv()

    def rs_go(i):
        hop = (i + 1) // 2
        for way in range(2):
            slot = RING // 2 + hop if way == 0 else RING // 2 - hop
            b = (i + way) % 2
            value = part[slot, b * half_r:(b + 1) * half_r, :]
            if i >= 2:
                rs_wait(i - 2, way)
                value += rs_recv[way, i - 2].astype(jnp.float32)
            rs_send[way, i] = value.astype(jnp.bfloat16)
            sent.append(push(
                rs_send.at[way, i], rs_recv.at[way, i], rs_out.at[way, i], rs_in.at[way, i],
                ways[way],
            ))

    project(RING // 2)
    rs_go(0)
    for hop in range(1, RING // 2):
        project(RING // 2 + hop)
        project(RING // 2 - hop)
        rs_go(2 * hop - 1)
        if hop == RING // 2 - 1:
            project(0)
        rs_go(2 * hop)
    for i in (last - 1, last):
        for way in range(2):
            b = (i + way) % 2
            rs_wait(i, way)
            part[0, b * half_r:(b + 1) * half_r, :] += rs_recv[way, i].astype(jnp.float32)
    out_ref[...] = part[0].astype(out_ref.dtype)
    for copy in sent:
        copy.wait_send()


def on_ring(tokens, positions, q_weight, kv_weight, o_weight):
    rows, width = tokens.shape
    piece = rows // RING
    hops = RING - 1
    any_space = pl.BlockSpec(memory_space=pltpu.HBM)
    vmem = pl.BlockSpec(memory_space=pltpu.VMEM)
    bf16, f32 = jnp.bfloat16, jnp.float32
    dma = pltpu.SemaphoreType.DMA
    return pl.pallas_call(
        fused,
        out_shape=jax.ShapeDtypeStruct((rows, width), bf16),
        in_specs=[any_space] * 5,
        out_specs=vmem,
        scratch_shapes=[
            pltpu.VMEM((1, rows), jnp.int32),
            pltpu.VMEM((RING, piece, HD), f32),
            pltpu.VMEM((RING, piece, HD), f32),
            pltpu.VMEM((RING, 2, rows, width // 2), bf16),
            pltpu.VMEM((RING, width, 2 * HD), bf16),
            pltpu.VMEM((width, 2 * HD), bf16),
            pltpu.VMEM((RING, 2 * HD, width), bf16),
            pltpu.VMEM((rows, 2 * HD), f32),
            pltpu.VMEM((rows, HD), f32),
            pltpu.VMEM((rows, HD), f32),
            pltpu.VMEM((2, rows, HD), f32),
            pltpu.VMEM((rows, HD), f32),
            pltpu.VMEM((RING, piece, HD), f32),
            pltpu.VMEM((RING, piece, HD), f32),
            pltpu.VMEM((2, RING, piece, HD), bf16),
            pltpu.VMEM((2, rows, HD), bf16),
            pltpu.VMEM((RING, rows, width), f32),
            pltpu.VMEM((2, hops, rows // 2, width), bf16),
            pltpu.VMEM((2, hops, rows // 2, width), bf16),
            dma, dma((2,)), dma, dma((RING,)), dma((RING,)), dma((RING,)),
            dma((RING,)), dma((RING,)), dma((RING,)),
            dma((2, hops)), dma((2, hops)), dma((3,)), dma((3,)),
            dma((RING,)), dma((RING,)), dma((2, RING)), dma((2, RING)),
            dma((2, hops)), dma((2, hops)),
        ],
        compiler_params=pltpu.CompilerParams(
            collective_id=0, has_side_effects=True, vmem_limit_bytes=60 * 2**20
        ),
        name="prefill_ring",
    )(
        positions[None, :], tokens, q_weight.reshape(RING, CORES, width, HD), kv_weight, o_weight,
    )


def solution(mesh):
    ring = mesh.shape["head"] == RING * CORES
    return jax.shard_map(
        on_ring if ring else on_device,
        mesh=mesh,
        in_specs=(P("grp", "head"), P("grp"), P(None, "head"), P("head", None), P("head", None)),
        out_specs=P("grp", "head"),
        check_vma=False,
    )
```

```python
import math

import jax
import jax.numpy as jnp
from jax import lax
from jax.experimental import pallas as pl
from jax.experimental.pallas import tpu as pltpu
from jax.sharding import PartitionSpec as P

HD = 128
GROUP = 16


def rotate(vals, positions):
    half = vals.shape[-1] // 2
    inverse = 500000.0 ** (-(jnp.arange(half, dtype=jnp.float32) * 2.0 / vals.shape[-1]))
    angles = positions.astype(jnp.float32)[:, None] * inverse[None, :]
    cosine = jnp.cos(angles)[:, None, :]
    sine = jnp.sin(angles)[:, None, :]
    first = vals[..., :half]
    second = vals[..., half:]
    return jnp.concatenate(
        [first * cosine - second * sine, second * cosine + first * sine], axis=-1
    )


def on_device(tokens, positions, q_weight, kv_weight, o_weight):
    count_tok = tokens.shape[0]
    width = q_weight.shape[1]
    head_size = HD
    local_heads = width // head_size
    kv_width = kv_weight.shape[1]
    kv_half = kv_width // 2
    first_head = lax.axis_index("head") * local_heads
    kv_index = first_head // GROUP
    q_raw = jnp.dot(
        lax.all_gather(tokens, "head", axis=1, tiled=True),
        q_weight,
        preferred_element_type=jnp.float32,
    )
    partial_value = jnp.dot(tokens, kv_weight, preferred_element_type=jnp.float32)
    kv_raw = lax.psum(partial_value, "head")
    k_raw = lax.dynamic_slice_in_dim(kv_raw, kv_index * head_size, head_size, 1)
    v_raw = lax.dynamic_slice_in_dim(kv_raw, kv_half + kv_index * head_size, head_size, 1)
    queries = rotate(q_raw.reshape(count_tok, local_heads, head_size), positions).astype(
        jnp.bfloat16
    )
    keys = rotate(k_raw.reshape(count_tok, 1, head_size), positions)[:, 0, :].astype(jnp.bfloat16)
    values = v_raw.astype(jnp.bfloat16)
    scores = jnp.einsum(
        "qhd,kd->hqk", queries, keys, preferred_element_type=jnp.float32
    ) / jnp.sqrt(jnp.float32(head_size))
    allowed = positions[None, :] <= positions[:, None]
    scores = jnp.where(allowed[None], scores, -1e30)
    peak = jnp.max(scores, axis=-1, keepdims=True)
    expo = jnp.where(allowed[None], jnp.exp(scores - peak), 0.0)
    weights = (expo / jnp.sum(expo, axis=-1, keepdims=True)).astype(jnp.bfloat16)
    context = jnp.einsum("hqk,kd->qhd", weights, values, preferred_element_type=jnp.float32)
    context = context.astype(jnp.bfloat16).reshape(count_tok, width)
    summed = lax.psum_scatter(
        lax.dot_general(
            o_weight, context, (((0,), (1,)), ((), ())), preferred_element_type=jnp.float32
        ),
        "head",
        scatter_dimension=0,
        tiled=True,
    ).T
    return summed.astype(jnp.bfloat16)


RING = 8
CORES = 2


def head_at(place, core):
    side = lax.div(place, RING // 2)
    level = place * (1 - side) + (RING - 1 - place) * side
    return (level * 2 + side) * CORES + core


def fused(
    pos_hbm, tok_hbm, q_hbm, kv_hbm, o_hbm, out_ref, pos, cos_ref, sin_ref,
    tok, tok_own, qw, kvw, ow, q_acc, q_send, q_recv, kv_part, kv_sib, kv_sum, kv_in, kv_all,
    ctx, part, rs_send, rs_recv,
    pos_sem, tok_sem, kvw_sem, q_sem, q_out, q_in, o_sem, o_out, o_in,
    ag_out, ag_in, pair_out, pair_in, qp_out, qp_in, cp_out, cp_in,
    kr_out, kr_in, ka_out, ka_in, rs_out, rs_in,
):
    rows, width = out_ref.shape
    half_w = width // 2
    half_r = rows // 2
    piece = rows // RING
    me = lax.axis_index("head")
    core = lax.rem(me, CORES)
    chip = lax.div(me, CORES)
    side = lax.rem(chip, 2)
    level = lax.div(chip, 2)
    place = level * (1 - side) + (RING - 1 - level) * side

    def at(offset, which):
        return head_at(lax.rem(place + offset + RING, RING), which)

    sibling = chip * CORES + (1 - core)
    right = at(1, core)
    left = at(-1, core)

    def push(src, dst, send, recv, target):
        copy = pltpu.make_async_remote_copy(
            src_ref=src, dst_ref=dst, send_sem=send, recv_sem=recv,
            device_id={"head": target}, device_id_type=pl.DeviceIdType.MESH,
        )
        copy.start()
        return copy

    def pull(src, dst, sem):
        copy = pltpu.make_async_copy(src, dst, sem)
        copy.start()
        return copy

    sent = []
    pos_local = pull(pos_hbm, pos, pos_sem)
    tok_local = pull(tok_hbm, tok_own, tok_sem)
    kvw_local = pull(kv_hbm, kvw, kvw_sem)

    barrier = pltpu.get_barrier_semaphore()
    for target in [sibling] + [at(offset, core) for offset in range(1, RING)]:
        pl.semaphore_signal(
            barrier, inc=1, device_id={"head": target}, device_id_type=pl.DeviceIdType.MESH
        )
    pl.semaphore_wait(barrier, RING)

    ways = (right, left)

    def shard(way, hop):
        return hop if way == 0 else (RING - hop) % RING

    def ag_send(h, i):
        for way in range(2):
            b = (i + way) % 2
            hop = i // 2
            if hop == 0:
                source = tok_hbm.at[pl.ds(h * half_r, half_r), pl.ds(b * half_w, half_w)]
            else:
                source = tok.at[h, shard(way, hop), b]
            sent.append(push(
                source, tok.at[h, shard(way, hop + 1), b],
                ag_out.at[h, way, i], ag_in.at[h, way, i], ways[way],
            ))

    def arrived(slot, send, recv, way):
        pltpu.make_async_remote_copy(
            src_ref=slot, dst_ref=slot, send_sem=send, recv_sem=recv,
            device_id={"head": ways[1 - way]}, device_id_type=pl.DeviceIdType.MESH,
        ).wait_recv()

    last = 2 * (RING // 2 - 1)

    def ag_step(h, i):
        for way in range(2):
            slot = tok.at[h, shard(way, i // 2 + 1), (i + way) % 2]
            arrived(slot, ag_out.at[h, way, i], ag_in.at[h, way, i], way)
        if i + 2 <= last:
            ag_send(h, i + 2)
        elif h == 0:
            ag_send(1, i + 1 - last)

    def q_add(h, i):
        for way in range(2):
            b = (i + way) % 2
            slot = shard(way, i // 2 + 1)
            q_acc[h] += jnp.dot(
                tok[h, slot, b], qw[slot, b * half_w:(b + 1) * half_w, :],
                preferred_element_type=jnp.float32,
            )

    ag_send(0, 0)
    ag_send(0, 1)

    q_local, q_pair = [], []
    for r in range(RING):
        owner = lax.div(at(-r, core), CORES)
        q_local.append(pull(q_hbm.at[owner, core], qw.at[r, :, 0:HD], q_sem.at[r]))
        q_pair.append(push(
            q_hbm.at[owner, 1 - core], qw.at[r, :, HD:2 * HD], q_out.at[r], q_in.at[r], sibling
        ))
    sent += q_pair

    tok_local.wait()
    kvw_local.wait()
    both = jnp.dot(tok_own[...], kvw[...], preferred_element_type=jnp.float32)
    kv_part[0] = both[:, 0:HD]
    kv_part[1] = both[:, HD:2 * HD]
    kv_pair = push(kv_part.at[1 - core], kv_sib, pair_out.at[0], pair_in.at[0], sibling)
    sent.append(kv_pair)

    ag_step(0, 0)

    pos_local.wait()
    pos_row = jnp.broadcast_to(pos[...].astype(jnp.float32), (rows, rows))
    pos_col = pos_row.T
    lane = lax.broadcasted_iota(jnp.int32, (rows, HD), 1)
    angle_step = lax.rem(lane, HD // 2).astype(jnp.float32) * (2.0 / HD)
    angles = pos_col * jnp.exp(angle_step * -math.log(500000.0))
    sine = jnp.sin(angles)
    cos_ref[...] = jnp.cos(angles).reshape(RING, piece, HD)
    sin_ref[...] = jnp.where(lane < HD // 2, -sine, sine).reshape(RING, piece, HD)

    ag_step(0, 1)
    kv_pair.wait_recv()
    kv_sum[...] = (kv_part[core] + kv_sib[...]).reshape(RING, piece, HD)
    kv_rows = []
    for r in range(1, RING):
        to = lax.rem(place + r, RING)
        kv_rows.append(push(
            kv_sum.at[to], kv_in.at[r], kr_out.at[r], kr_in.at[r], at(r, core)
        ))
    sent += kv_rows

    o_local, o_pair = [], []
    for r in range(RING):
        mine = pl.multiple_of(at(-r, core) * width, width)
        theirs = pl.multiple_of(at(-r, 1 - core) * width, width)
        o_local.append(pull(o_hbm.at[:, pl.ds(mine, width)], ow.at[r, 0:HD], o_sem.at[r]))
        o_pair.append(push(
            o_hbm.at[:, pl.ds(theirs, width)], ow.at[r, HD:2 * HD], o_out.at[r], o_in.at[r],
            sibling,
        ))
    sent += o_pair

    ag_step(0, 2)
    for r in range(RING):
        q_local[r].wait()
        q_pair[r].wait_recv()
    own = jnp.dot(tok_own[...], qw[0], preferred_element_type=jnp.float32)
    q_acc[0] = own[:half_r]
    q_acc[1] = own[half_r:]
    ag_step(0, 3)
    for i in range(3):
        q_add(0, i)
    total = kv_sum[place]
    for r in range(1, RING):
        kv_rows[r - 1].wait_recv()
        total += kv_in[r]
    turned = total * cos_ref[place] + pltpu.roll(total, HD // 2, 1) * sin_ref[place]
    is_key = (core == 0).astype(jnp.float32)
    kv_all[core, place] = (turned * is_key + total * (1.0 - is_key)).astype(jnp.bfloat16)
    kv_out = []
    for r in range(1, RING):
        kv_out.append(push(
            kv_all.at[core, place], kv_all.at[core, place], ka_out.at[r], ka_in.at[r], at(r, core)
        ))
    sent += kv_out
    ag_step(0, 4)
    q_add(0, 3)
    q_add(0, 4)
    ag_step(0, 5)
    q_add(0, 5)
    for copy in kv_out:
        copy.wait_recv()
    kv_pass = push(kv_all.at[core], kv_all.at[core], pair_out.at[1], pair_in.at[1], sibling)
    sent.append(kv_pass)
    ag_step(0, 6)
    q_add(0, 6)

    def q_exchange(h):
        q_send[h] = q_acc[h, :, HD:2 * HD]
        copy = push(q_send.at[h], q_recv.at[h], qp_out.at[h], qp_in.at[h], sibling)
        sent.append(copy)
        return copy

    def attend(h, q_pass):
        q_pass.wait_recv()
        lines = slice(h * half_r, (h + 1) * half_r)
        q_raw = q_acc[h, :, 0:HD] + q_recv[h]
        cosine = cos_ref[h * RING // 2:(h + 1) * RING // 2].reshape(half_r, HD)
        sine = sin_ref[h * RING // 2:(h + 1) * RING // 2].reshape(half_r, HD)
        queries = (q_raw * cosine + pltpu.roll(q_raw, HD // 2, 1) * sine).astype(jnp.bfloat16)
        keys = kv_all[0].reshape(rows, HD)
        values = kv_all[1].reshape(rows, HD)
        scores = lax.dot_general(
            queries, keys, (((1,), (1,)), ((), ())), preferred_element_type=jnp.float32
        ) * (HD ** -0.5)
        allowed = pos_row[lines] <= pos_col[lines]
        scores = jnp.where(allowed, scores, -1e30)
        peak = jnp.max(scores, axis=-1, keepdims=True)
        expo = jnp.where(allowed, jnp.exp(scores - peak), 0.0)
        weights = (expo / jnp.sum(expo, axis=-1, keepdims=True)).astype(jnp.bfloat16)
        ctx[h, 0] = jnp.dot(
            weights, values, preferred_element_type=jnp.float32
        ).astype(jnp.bfloat16)
        copy = push(ctx.at[h, 0], ctx.at[h, 1], cp_out.at[h], cp_in.at[h], sibling)
        sent.append(copy)
        return copy

    tile = 2 * HD

    def project(h, slot):
        context = jnp.concatenate([ctx[h, 0], ctx[h, 1]], axis=1)
        for n in range(width // tile):
            b, start = divmod(n * tile, half_w)
            part[h, slot, b, :, start:start + tile] = jnp.dot(
                context, ow[slot, :, n * tile:(n + 1) * tile], preferred_element_type=jnp.float32
            )

    def rs_wait(h, i, way):
        arrived(rs_recv.at[h, way, i], rs_out.at[h, way, i], rs_in.at[h, way, i], way)

    def rs_go(h, i):
        hop = (i + 1) // 2
        if i == 0:
            project(h, RING // 2)
        elif i % 2:
            project(h, RING // 2 + hop)
            project(h, RING // 2 - hop)
        for way in range(2):
            slot = RING // 2 + hop if way == 0 else RING // 2 - hop
            b = (i + way) % 2
            value = part[h, slot, b]
            if i >= 2:
                rs_wait(h, i - 2, way)
                value += rs_recv[h, way, i - 2].astype(jnp.float32)
            rs_send[h, way, i] = value.astype(jnp.bfloat16)
            sent.append(push(
                rs_send.at[h, way, i], rs_recv.at[h, way, i],
                rs_out.at[h, way, i], rs_in.at[h, way, i], ways[way],
            ))

    def rs_end(h):
        for i in (last - 1, last):
            for way in range(2):
                b = (i + way) % 2
                rs_wait(h, i, way)
                part[h, 0, b] += rs_recv[h, way, i].astype(jnp.float32)
        for b in range(2):
            out_ref[h * half_r:(h + 1) * half_r, b * half_w:(b + 1) * half_w] = (
                part[h, 0, b].astype(out_ref.dtype)
            )

    q_pass = q_exchange(0)
    ag_step(1, 0)
    q_add(1, 0)
    kv_pass_in = kv_all.at[1 - core]
    pltpu.make_async_remote_copy(
        src_ref=kv_pass_in, dst_ref=kv_pass_in, send_sem=pair_out.at[1], recv_sem=pair_in.at[1],
        device_id={"head": sibling}, device_id_type=pl.DeviceIdType.MESH,
    ).wait_recv()
    ctx_pass = attend(0, q_pass)
    ag_step(1, 1)
    q_add(1, 1)
    for r in range(RING):
        o_local[r].wait()
        o_pair[r].wait_recv()
    ctx_pass.wait_recv()
    rs_go(0, 0)
    ag_step(1, 2)
    rs_go(0, 1)
    q_add(1, 2)
    ag_step(1, 3)
    q_add(1, 3)
    ag_step(1, 4)
    rs_go(0, 2)
    q_add(1, 4)
    ag_step(1, 5)
    q_add(1, 5)
    rs_go(0, 3)
    ag_step(1, 6)
    q_add(1, 6)
    q_pass = q_exchange(1)
    rs_go(0, 4)
    ctx_pass = attend(1, q_pass)
    rs_go(0, 5)
    ctx_pass.wait_recv()
    rs_go(1, 0)
    rs_go(0, 6)
    rs_go(1, 1)
    project(0, 0)
    rs_go(1, 2)
    rs_go(1, 3)
    rs_end(0)
    rs_go(1, 4)
    rs_go(1, 5)
    project(1, 0)
    rs_go(1, 6)
    rs_end(1)
    for copy in sent:
        copy.wait_send()


def on_ring(tokens, positions, q_weight, kv_weight, o_weight):
    rows, width = tokens.shape
    piece = rows // RING
    hops = RING - 1
    any_space = pl.BlockSpec(memory_space=pltpu.HBM)
    vmem = pl.BlockSpec(memory_space=pltpu.VMEM)
    bf16, f32 = jnp.bfloat16, jnp.float32
    dma = pltpu.SemaphoreType.DMA
    return pl.pallas_call(
        fused,
        out_shape=jax.ShapeDtypeStruct((rows, width), bf16),
        in_specs=[any_space] * 5,
        out_specs=vmem,
        scratch_shapes=[
            pltpu.VMEM((1, rows), jnp.int32),
            pltpu.VMEM((RING, piece, HD), f32),
            pltpu.VMEM((RING, piece, HD), f32),
            pltpu.VMEM((2, RING, 2, rows // 2, width // 2), bf16),
            pltpu.VMEM((rows, width), bf16),
            pltpu.VMEM((RING, width, 2 * HD), bf16),
            pltpu.VMEM((width, 2 * HD), bf16),
            pltpu.VMEM((RING, 2 * HD, width), bf16),
            pltpu.VMEM((2, rows // 2, 2 * HD), f32),
            pltpu.VMEM((2, rows // 2, HD), f32),
            pltpu.VMEM((2, rows // 2, HD), f32),
            pltpu.VMEM((2, rows, HD), f32),
            pltpu.VMEM((rows, HD), f32),
            pltpu.VMEM((RING, piece, HD), f32),
            pltpu.VMEM((RING, piece, HD), f32),
            pltpu.VMEM((2, RING, piece, HD), bf16),
            pltpu.VMEM((2, 2, rows // 2, HD), bf16),
            pltpu.VMEM((2, RING, 2, rows // 2, width // 2), f32),
            pltpu.VMEM((2, 2, hops, rows // 2, width // 2), bf16),
            pltpu.VMEM((2, 2, hops, rows // 2, width // 2), bf16),
            dma, dma, dma, dma((RING,)), dma((RING,)), dma((RING,)),
            dma((RING,)), dma((RING,)), dma((RING,)),
            dma((2, 2, hops)), dma((2, 2, hops)), dma((2,)), dma((2,)),
            dma((2,)), dma((2,)), dma((2,)), dma((2,)),
            dma((RING,)), dma((RING,)), dma((RING,)), dma((RING,)),
            dma((2, 2, hops)), dma((2, 2, hops)),
        ],
        compiler_params=pltpu.CompilerParams(
            collective_id=0, has_side_effects=True, vmem_limit_bytes=40 * 2**20
        ),
        name="prefill_ring",
    )(
        positions[None, :], tokens, q_weight.reshape(RING, CORES, width, HD), kv_weight, o_weight,
    )


def solution(mesh):
    ring = mesh.shape["head"] == RING * CORES
    return jax.shard_map(
        on_ring if ring else on_device,
        mesh=mesh,
        in_specs=(P("grp", "head"), P("grp"), P(None, "head"), P("head", None), P("head", None)),
        out_specs=P("grp", "head"),
        check_vma=False,
    )
```

```python
import math

import jax
import jax.numpy as jnp
from jax import lax
from jax.experimental import pallas as pl
from jax.experimental.pallas import tpu as pltpu
from jax.sharding import PartitionSpec as P

HD = 128
GROUP = 16


def rotate(vals, positions):
    half = vals.shape[-1] // 2
    inverse = 500000.0 ** (-(jnp.arange(half, dtype=jnp.float32) * 2.0 / vals.shape[-1]))
    angles = positions.astype(jnp.float32)[:, None] * inverse[None, :]
    cosine = jnp.cos(angles)[:, None, :]
    sine = jnp.sin(angles)[:, None, :]
    first = vals[..., :half]
    second = vals[..., half:]
    return jnp.concatenate(
        [first * cosine - second * sine, second * cosine + first * sine], axis=-1
    )


def on_device(tokens, positions, q_weight, kv_weight, o_weight):
    count_tok = tokens.shape[0]
    width = q_weight.shape[1]
    head_size = HD
    local_heads = width // head_size
    kv_width = kv_weight.shape[1]
    kv_half = kv_width // 2
    first_head = lax.axis_index("head") * local_heads
    kv_index = first_head // GROUP
    q_raw = jnp.dot(
        lax.all_gather(tokens, "head", axis=1, tiled=True),
        q_weight,
        preferred_element_type=jnp.float32,
    )
    partial_value = jnp.dot(tokens, kv_weight, preferred_element_type=jnp.float32)
    kv_raw = lax.psum(partial_value, "head")
    k_raw = lax.dynamic_slice_in_dim(kv_raw, kv_index * head_size, head_size, 1)
    v_raw = lax.dynamic_slice_in_dim(kv_raw, kv_half + kv_index * head_size, head_size, 1)
    queries = rotate(q_raw.reshape(count_tok, local_heads, head_size), positions).astype(
        jnp.bfloat16
    )
    keys = rotate(k_raw.reshape(count_tok, 1, head_size), positions)[:, 0, :].astype(jnp.bfloat16)
    values = v_raw.astype(jnp.bfloat16)
    scores = jnp.einsum(
        "qhd,kd->hqk", queries, keys, preferred_element_type=jnp.float32
    ) / jnp.sqrt(jnp.float32(head_size))
    allowed = positions[None, :] <= positions[:, None]
    scores = jnp.where(allowed[None], scores, -1e30)
    peak = jnp.max(scores, axis=-1, keepdims=True)
    expo = jnp.where(allowed[None], jnp.exp(scores - peak), 0.0)
    weights = (expo / jnp.sum(expo, axis=-1, keepdims=True)).astype(jnp.bfloat16)
    context = jnp.einsum("hqk,kd->qhd", weights, values, preferred_element_type=jnp.float32)
    context = context.astype(jnp.bfloat16).reshape(count_tok, width)
    summed = lax.psum_scatter(
        lax.dot_general(
            o_weight, context, (((0,), (1,)), ((), ())), preferred_element_type=jnp.float32
        ),
        "head",
        scatter_dimension=0,
        tiled=True,
    ).T
    return summed.astype(jnp.bfloat16)


RING = 8
CORES = 2


def head_at(place, core):
    side = lax.div(place, RING // 2)
    level = place * (1 - side) + (RING - 1 - place) * side
    return (level * 2 + side) * CORES + core


def fused(
    pos_hbm, tok_hbm, q_hbm, kv_hbm, o_hbm, out_ref, pos, cos_ref, sin_ref,
    tok, tok_own, qw, kvw, ow, q_acc, q_send, q_recv, kv_part, kv_sib, kv_sum, kv_in, kv_all,
    ctx, part, rs_send, rs_recv,
    pos_sem, tok_sem, kvw_sem, q_sem, q_out, q_in, o_sem, o_out, o_in,
    ag_out, ag_in, pair_out, pair_in, qp_out, qp_in, cp_out, cp_in,
    kr_out, kr_in, ka_out, ka_in, rs_out, rs_in,
):
    rows, width = out_ref.shape
    half_w = width // 2
    half_r = rows // 2
    piece = rows // RING
    me = lax.axis_index("head")
    core = lax.rem(me, CORES)
    chip = lax.div(me, CORES)
    side = lax.rem(chip, 2)
    level = lax.div(chip, 2)
    place = level * (1 - side) + (RING - 1 - level) * side

    def at(offset, which):
        return head_at(lax.rem(place + offset + RING, RING), which)

    sibling = chip * CORES + (1 - core)
    right = at(1, core)
    left = at(-1, core)

    def push(src, dst, send, recv, target):
        copy = pltpu.make_async_remote_copy(
            src_ref=src, dst_ref=dst, send_sem=send, recv_sem=recv,
            device_id={"head": target}, device_id_type=pl.DeviceIdType.MESH,
        )
        copy.start()
        return copy

    def pull(src, dst, sem):
        copy = pltpu.make_async_copy(src, dst, sem)
        copy.start()
        return copy

    sent = []
    pos_local = pull(pos_hbm, pos, pos_sem)
    tok_local = pull(tok_hbm, tok_own, tok_sem)
    kvw_local = pull(kv_hbm, kvw, kvw_sem)

    barrier = pltpu.get_barrier_semaphore()
    for target in [sibling] + [at(offset, core) for offset in range(1, RING)]:
        pl.semaphore_signal(
            barrier, inc=1, device_id={"head": target}, device_id_type=pl.DeviceIdType.MESH
        )
    pl.semaphore_wait(barrier, RING)

    ways = (right, left)

    def shard(way, hop):
        return hop if way == 0 else (RING - hop) % RING

    def ag_send(h, i):
        for way in range(2):
            b = (i + way) % 2
            hop = i // 2
            if hop == 0:
                source = tok_hbm.at[pl.ds(h * half_r, half_r), pl.ds(b * half_w, half_w)]
            else:
                source = tok.at[h, shard(way, hop), b]
            sent.append(push(
                source, tok.at[h, shard(way, hop + 1), b],
                ag_out.at[h, way, i], ag_in.at[h, way, i], ways[way],
            ))

    def arrived(slot, send, recv, way):
        pltpu.make_async_remote_copy(
            src_ref=slot, dst_ref=slot, send_sem=send, recv_sem=recv,
            device_id={"head": ways[1 - way]}, device_id_type=pl.DeviceIdType.MESH,
        ).wait_recv()

    last = 2 * (RING // 2 - 1)

    def ag_step(h, i):
        for way in range(2):
            slot = tok.at[h, shard(way, i // 2 + 1), (i + way) % 2]
            arrived(slot, ag_out.at[h, way, i], ag_in.at[h, way, i], way)
        if i + 2 <= last:
            ag_send(h, i + 2)
        elif h == 0:
            ag_send(1, i + 1 - last)

    def q_add(h, i):
        for way in range(2):
            b = (i + way) % 2
            slot = shard(way, i // 2 + 1)
            q_acc[h] += jnp.dot(
                tok[h, slot, b], qw[slot, b * half_w:(b + 1) * half_w, :],
                preferred_element_type=jnp.float32,
            )

    ag_send(0, 0)
    ag_send(0, 1)

    q_local, q_pair = [], []
    for r in range(RING):
        owner = lax.div(at(-r, core), CORES)
        q_local.append(pull(q_hbm.at[owner, core], qw.at[r, :, 0:HD], q_sem.at[r]))
        q_pair.append(push(
            q_hbm.at[owner, 1 - core], qw.at[r, :, HD:2 * HD], q_out.at[r], q_in.at[r], sibling
        ))
    sent += q_pair

    tok_local.wait()
    kvw_local.wait()
    both = jnp.dot(tok_own[...], kvw[...], preferred_element_type=jnp.float32)
    kv_part[0] = both[:, 0:HD]
    kv_part[1] = both[:, HD:2 * HD]
    kv_pair = push(kv_part.at[1 - core], kv_sib, pair_out.at[0], pair_in.at[0], sibling)
    sent.append(kv_pair)

    ag_step(0, 0)

    pos_local.wait()
    pos_row = jnp.broadcast_to(pos[...].astype(jnp.float32), (rows, rows))
    pos_col = pos_row.T
    lane = lax.broadcasted_iota(jnp.int32, (rows, HD), 1)
    angle_step = lax.rem(lane, HD // 2).astype(jnp.float32) * (2.0 / HD)
    angles = pos_col * jnp.exp(angle_step * -math.log(500000.0))
    sine = jnp.sin(angles)
    cos_ref[...] = jnp.cos(angles).reshape(RING, piece, HD)
    sin_ref[...] = jnp.where(lane < HD // 2, -sine, sine).reshape(RING, piece, HD)

    ag_step(0, 1)
    kv_pair.wait_recv()
    kv_sum[...] = (kv_part[core] + kv_sib[...]).reshape(RING, piece, HD)
    kv_rows = []
    for r in range(1, RING):
        to = lax.rem(place + r, RING)
        kv_rows.append(push(
            kv_sum.at[to], kv_in.at[r], kr_out.at[r], kr_in.at[r], at(r, core)
        ))
    sent += kv_rows

    o_local, o_pair = [], []
    for r in range(RING):
        mine = pl.multiple_of(at(-r, core) * width, width)
        theirs = pl.multiple_of(at(-r, 1 - core) * width, width)
        o_local.append(pull(o_hbm.at[:, pl.ds(mine, width)], ow.at[r, 0:HD], o_sem.at[r]))
        o_pair.append(push(
            o_hbm.at[:, pl.ds(theirs, width)], ow.at[r, HD:2 * HD], o_out.at[r], o_in.at[r],
            sibling,
        ))
    sent += o_pair

    ag_step(0, 2)
    for r in range(RING):
        q_local[r].wait()
        q_pair[r].wait_recv()
    own = jnp.dot(tok_own[...], qw[0], preferred_element_type=jnp.float32)
    q_acc[0] = own[:half_r]
    q_acc[1] = own[half_r:]
    ag_step(0, 3)
    for i in range(3):
        q_add(0, i)
    total = kv_sum[place]
    for r in range(1, RING):
        kv_rows[r - 1].wait_recv()
        total += kv_in[r]
    turned = total * cos_ref[place] + pltpu.roll(total, HD // 2, 1) * sin_ref[place]
    is_key = (core == 0).astype(jnp.float32)
    kv_all[core, place] = (turned * is_key + total * (1.0 - is_key)).astype(jnp.bfloat16)
    kv_out = []
    for r in range(1, RING):
        kv_out.append(push(
            kv_all.at[core, place], kv_all.at[core, place], ka_out.at[r], ka_in.at[r], at(r, core)
        ))
    sent += kv_out
    ag_step(0, 4)
    q_add(0, 3)
    q_add(0, 4)
    ag_step(0, 5)
    q_add(0, 5)
    for copy in kv_out:
        copy.wait_recv()
    kv_pass = push(kv_all.at[core], kv_all.at[core], pair_out.at[1], pair_in.at[1], sibling)
    sent.append(kv_pass)
    ag_step(0, 6)
    q_add(0, 6)

    def q_exchange(h):
        q_send[h] = q_acc[h, :, HD:2 * HD]
        copy = push(q_send.at[h], q_recv.at[h], qp_out.at[h], qp_in.at[h], sibling)
        sent.append(copy)
        return copy

    def attend(h, q_pass):
        q_pass.wait_recv()
        lines = slice(h * half_r, (h + 1) * half_r)
        q_raw = q_acc[h, :, 0:HD] + q_recv[h]
        cosine = cos_ref[h * RING // 2:(h + 1) * RING // 2].reshape(half_r, HD)
        sine = sin_ref[h * RING // 2:(h + 1) * RING // 2].reshape(half_r, HD)
        queries = (q_raw * cosine + pltpu.roll(q_raw, HD // 2, 1) * sine).astype(jnp.bfloat16)
        keys = kv_all[0].reshape(rows, HD)
        values = kv_all[1].reshape(rows, HD)
        scores = lax.dot_general(
            queries, keys, (((1,), (1,)), ((), ())), preferred_element_type=jnp.float32
        ) * (HD ** -0.5)
        allowed = pos_row[lines] <= pos_col[lines]
        scores = jnp.where(allowed, scores, -1e30)
        peak = jnp.max(scores, axis=-1, keepdims=True)
        expo = jnp.where(allowed, jnp.exp(scores - peak), 0.0)
        weights = (expo / jnp.sum(expo, axis=-1, keepdims=True)).astype(jnp.bfloat16)
        ctx[h, 0] = jnp.dot(
            weights, values, preferred_element_type=jnp.float32
        ).astype(jnp.bfloat16)
        copy = push(ctx.at[h, 0], ctx.at[h, 1], cp_out.at[h], cp_in.at[h], sibling)
        sent.append(copy)
        return copy

    tile = 2 * HD

    def project(h, slot):
        context = jnp.concatenate([ctx[h, 0], ctx[h, 1]], axis=1)
        for n in range(width // tile):
            b, start = divmod(n * tile, half_w)
            part[h, slot, b, :, start:start + tile] = jnp.dot(
                context, ow[slot, :, n * tile:(n + 1) * tile], preferred_element_type=jnp.float32
            )

    def rs_wait(h, i, way):
        arrived(rs_recv.at[h, way, i], rs_out.at[h, way, i], rs_in.at[h, way, i], way)

    def rs_go(h, i):
        hop = (i + 1) // 2
        if i == 0:
            project(h, RING // 2)
        elif i % 2:
            project(h, RING // 2 + hop)
            project(h, RING // 2 - hop)
        for way in range(2):
            slot = RING // 2 + hop if way == 0 else RING // 2 - hop
            b = (i + way) % 2
            value = part[h, slot, b]
            if i >= 2:
                rs_wait(h, i - 2, way)
                value += rs_recv[h, way, i - 2].astype(jnp.float32)
            rs_send[h, way, i] = value.astype(jnp.bfloat16)
            sent.append(push(
                rs_send.at[h, way, i], rs_recv.at[h, way, i],
                rs_out.at[h, way, i], rs_in.at[h, way, i], ways[way],
            ))

    def rs_end(h):
        for i in (last - 1, last):
            for way in range(2):
                b = (i + way) % 2
                rs_wait(h, i, way)
                part[h, 0, b] += rs_recv[h, way, i].astype(jnp.float32)
        for b in range(2):
            out_ref[h * half_r:(h + 1) * half_r, b * half_w:(b + 1) * half_w] = (
                part[h, 0, b].astype(out_ref.dtype)
            )

    q_pass = q_exchange(0)
    ag_step(1, 0)
    q_add(1, 0)
    kv_pass_in = kv_all.at[1 - core]
    pltpu.make_async_remote_copy(
        src_ref=kv_pass_in, dst_ref=kv_pass_in, send_sem=pair_out.at[1], recv_sem=pair_in.at[1],
        device_id={"head": sibling}, device_id_type=pl.DeviceIdType.MESH,
    ).wait_recv()
    ctx_pass = attend(0, q_pass)
    ag_step(1, 1)
    q_add(1, 1)
    for r in range(RING):
        o_local[r].wait()
        o_pair[r].wait_recv()
    ctx_pass.wait_recv()
    rs_go(0, 0)
    ag_step(1, 2)
    rs_go(0, 1)
    q_add(1, 2)
    ag_step(1, 3)
    q_add(1, 3)
    ag_step(1, 4)
    rs_go(0, 2)
    q_add(1, 4)
    ag_step(1, 5)
    q_add(1, 5)
    rs_go(0, 3)
    ag_step(1, 6)
    q_add(1, 6)
    q_pass = q_exchange(1)
    rs_go(0, 4)
    ctx_pass = attend(1, q_pass)
    rs_go(0, 5)
    ctx_pass.wait_recv()
    rs_go(1, 0)
    rs_go(0, 6)
    rs_go(1, 1)
    project(0, 0)
    rs_go(1, 2)
    rs_go(1, 3)
    rs_end(0)
    rs_go(1, 4)
    rs_go(1, 5)
    project(1, 0)
    rs_go(1, 6)
    rs_end(1)
    for copy in sent:
        copy.wait_send()


def on_ring(tokens, positions, q_weight, kv_weight, o_weight):
    rows, width = tokens.shape
    piece = rows // RING
    hops = RING - 1
    any_space = pl.BlockSpec(memory_space=pltpu.HBM)
    vmem = pl.BlockSpec(memory_space=pltpu.VMEM)
    bf16, f32 = jnp.bfloat16, jnp.float32
    dma = pltpu.SemaphoreType.DMA
    return pl.pallas_call(
        fused,
        out_shape=jax.ShapeDtypeStruct((rows, width), bf16),
        in_specs=[any_space] * 5,
        out_specs=vmem,
        scratch_shapes=[
            pltpu.VMEM((1, rows), jnp.int32),
            pltpu.VMEM((RING, piece, HD), f32),
            pltpu.VMEM((RING, piece, HD), f32),
            pltpu.VMEM((2, RING, 2, rows // 2, width // 2), bf16),
            pltpu.VMEM((rows, width), bf16),
            pltpu.VMEM((RING, width, 2 * HD), bf16),
            pltpu.VMEM((width, 2 * HD), bf16),
            pltpu.VMEM((RING, 2 * HD, width), bf16),
            pltpu.VMEM((2, rows // 2, 2 * HD), f32),
            pltpu.VMEM((2, rows // 2, HD), f32),
            pltpu.VMEM((2, rows // 2, HD), f32),
            pltpu.VMEM((2, rows, HD), f32),
            pltpu.VMEM((rows, HD), f32),
            pltpu.VMEM((RING, piece, HD), f32),
            pltpu.VMEM((RING, piece, HD), f32),
            pltpu.VMEM((2, RING, piece, HD), bf16),
            pltpu.VMEM((2, 2, rows // 2, HD), bf16),
            pltpu.VMEM((2, RING, 2, rows // 2, width // 2), f32),
            pltpu.VMEM((2, 2, hops, rows // 2, width // 2), bf16),
            pltpu.VMEM((2, 2, hops, rows // 2, width // 2), bf16),
            dma, dma, dma, dma((RING,)), dma((RING,)), dma((RING,)),
            dma((RING,)), dma((RING,)), dma((RING,)),
            dma((2, 2, hops)), dma((2, 2, hops)), dma((2,)), dma((2,)),
            dma((2,)), dma((2,)), dma((2,)), dma((2,)),
            dma((RING,)), dma((RING,)), dma((RING,)), dma((RING,)),
            dma((2, 2, hops)), dma((2, 2, hops)),
        ],
        compiler_params=pltpu.CompilerParams(
            collective_id=0, has_side_effects=True, vmem_limit_bytes=60 * 2**20
        ),
        name="prefill_ring",
    )(
        positions[None, :], tokens, q_weight.reshape(RING, CORES, width, HD), kv_weight, o_weight,
    )


def solution(mesh):
    ring = mesh.shape["head"] == RING * CORES
    return jax.shard_map(
        on_ring if ring else on_device,
        mesh=mesh,
        in_specs=(P("grp", "head"), P("grp"), P(None, "head"), P("head", None), P("head", None)),
        out_specs=P("grp", "head"),
        check_vma=False,
    )
```

```python
import math

import jax
import jax.numpy as jnp
from jax import lax
from jax.experimental import pallas as pl
from jax.experimental.pallas import tpu as pltpu
from jax.sharding import PartitionSpec as P

HD = 128
GROUP = 16


def rotate(vals, positions):
    half = vals.shape[-1] // 2
    inverse = 500000.0 ** (-(jnp.arange(half, dtype=jnp.float32) * 2.0 / vals.shape[-1]))
    angles = positions.astype(jnp.float32)[:, None] * inverse[None, :]
    cosine = jnp.cos(angles)[:, None, :]
    sine = jnp.sin(angles)[:, None, :]
    first = vals[..., :half]
    second = vals[..., half:]
    return jnp.concatenate(
        [first * cosine - second * sine, second * cosine + first * sine], axis=-1
    )


def on_device(tokens, positions, q_weight, kv_weight, o_weight):
    count_tok = tokens.shape[0]
    width = q_weight.shape[1]
    head_size = HD
    local_heads = width // head_size
    kv_width = kv_weight.shape[1]
    kv_half = kv_width // 2
    first_head = lax.axis_index("head") * local_heads
    kv_index = first_head // GROUP
    q_raw = jnp.dot(
        lax.all_gather(tokens, "head", axis=1, tiled=True),
        q_weight,
        preferred_element_type=jnp.float32,
    )
    partial_value = jnp.dot(tokens, kv_weight, preferred_element_type=jnp.float32)
    kv_raw = lax.psum(partial_value, "head")
    k_raw = lax.dynamic_slice_in_dim(kv_raw, kv_index * head_size, head_size, 1)
    v_raw = lax.dynamic_slice_in_dim(kv_raw, kv_half + kv_index * head_size, head_size, 1)
    queries = rotate(q_raw.reshape(count_tok, local_heads, head_size), positions).astype(
        jnp.bfloat16
    )
    keys = rotate(k_raw.reshape(count_tok, 1, head_size), positions)[:, 0, :].astype(jnp.bfloat16)
    values = v_raw.astype(jnp.bfloat16)
    scores = jnp.einsum(
        "qhd,kd->hqk", queries, keys, preferred_element_type=jnp.float32
    ) / jnp.sqrt(jnp.float32(head_size))
    allowed = positions[None, :] <= positions[:, None]
    scores = jnp.where(allowed[None], scores, -1e30)
    peak = jnp.max(scores, axis=-1, keepdims=True)
    expo = jnp.where(allowed[None], jnp.exp(scores - peak), 0.0)
    weights = (expo / jnp.sum(expo, axis=-1, keepdims=True)).astype(jnp.bfloat16)
    context = jnp.einsum("hqk,kd->qhd", weights, values, preferred_element_type=jnp.float32)
    context = context.astype(jnp.bfloat16).reshape(count_tok, width)
    summed = lax.psum_scatter(
        lax.dot_general(
            o_weight, context, (((0,), (1,)), ((), ())), preferred_element_type=jnp.float32
        ),
        "head",
        scatter_dimension=0,
        tiled=True,
    ).T
    return summed.astype(jnp.bfloat16)


RING = 8
CORES = 2


def head_at(place, core):
    side = lax.div(place, RING // 2)
    level = place * (1 - side) + (RING - 1 - place) * side
    return (level * 2 + side) * CORES + core


def fused(
    pos_hbm, tok_hbm, q_hbm, kv_hbm, o_hbm, out_ref, pos, cos_ref, sin_ref,
    tok, qw, kvw, ow, q_acc, q_send, q_recv, kv_part, kv_sib, kv_sum, kv_in, kv_all,
    ctx, part, rs_send, rs_recv,
    pos_sem, tok_sem, kvw_sem, q_sem, q_out, q_in, o_sem, o_out, o_in,
    ag_out, ag_in, pair_out, pair_in, kr_out, kr_in, ka_out, ka_in, rs_out, rs_in,
):
    rows, width = out_ref.shape
    half_w = width // 2
    half_r = rows // 2
    piece = rows // RING
    me = lax.axis_index("head")
    core = lax.rem(me, CORES)
    chip = lax.div(me, CORES)
    side = lax.rem(chip, 2)
    level = lax.div(chip, 2)
    place = level * (1 - side) + (RING - 1 - level) * side

    def at(offset, which):
        return head_at(lax.rem(place + offset + RING, RING), which)

    sibling = chip * CORES + (1 - core)
    right = at(1, core)
    left = at(-1, core)

    def push(src, dst, send, recv, target):
        copy = pltpu.make_async_remote_copy(
            src_ref=src, dst_ref=dst, send_sem=send, recv_sem=recv,
            device_id={"head": target}, device_id_type=pl.DeviceIdType.MESH,
        )
        copy.start()
        return copy

    def pull(src, dst, sem):
        copy = pltpu.make_async_copy(src, dst, sem)
        copy.start()
        return copy

    sent = []
    pos_local = pull(pos_hbm, pos, pos_sem)
    tok_local = [
        pull(tok_hbm.at[:, pl.ds(b * half_w, half_w)], tok.at[0, b], tok_sem.at[b])
        for b in range(2)
    ]
    kvw_local = pull(kv_hbm, kvw, kvw_sem)

    barrier = pltpu.get_barrier_semaphore()
    for target in [sibling] + [at(offset, core) for offset in range(1, RING)]:
        pl.semaphore_signal(
            barrier, inc=1, device_id={"head": target}, device_id_type=pl.DeviceIdType.MESH
        )
    pl.semaphore_wait(barrier, RING)

    ways = (right, left)

    def shard(way, hop):
        return hop if way == 0 else (RING - hop) % RING

    def ag_send(i):
        for way in range(2):
            b = (i + way) % 2
            hop = i // 2
            if hop == 0:
                source = tok_hbm.at[:, pl.ds(b * half_w, half_w)]
            else:
                source = tok.at[shard(way, hop), b]
            sent.append(push(
                source, tok.at[shard(way, hop + 1), b],
                ag_out.at[way, i], ag_in.at[way, i], ways[way],
            ))

    def ag_wait(i, way):
        b = (i + way) % 2
        slot = tok.at[shard(way, i // 2 + 1), b]
        pltpu.make_async_remote_copy(
            src_ref=slot, dst_ref=slot, send_sem=ag_out.at[way, i], recv_sem=ag_in.at[way, i],
            device_id={"head": ways[1 - way]}, device_id_type=pl.DeviceIdType.MESH,
        ).wait_recv()

    def q_add(slot, b):
        q_acc[...] += jnp.dot(
            tok[slot, b], qw[slot, b * half_w:(b + 1) * half_w, :],
            preferred_element_type=jnp.float32,
        )

    last = 2 * (RING // 2 - 1)
    ag_send(0)
    ag_send(1)

    q_local, q_pair = [], []
    for r in range(RING):
        owner = lax.div(at(-r, core), CORES)
        q_local.append(pull(q_hbm.at[owner, core], qw.at[r, :, 0:HD], q_sem.at[r]))
        q_pair.append(push(
            q_hbm.at[owner, 1 - core], qw.at[r, :, HD:2 * HD], q_out.at[r], q_in.at[r], sibling
        ))
    sent += q_pair

    pos_local.wait()
    pos_row = jnp.broadcast_to(pos[...].astype(jnp.float32), (rows, rows))
    pos_col = pos_row.T
    allowed = pos_row <= pos_col
    lane = lax.broadcasted_iota(jnp.int32, (rows, HD), 1)
    angle_step = lax.rem(lane, HD // 2).astype(jnp.float32) * (2.0 / HD)
    angles = pos_col * jnp.exp(angle_step * -math.log(500000.0))
    sine = jnp.sin(angles)
    cos_ref[...] = jnp.cos(angles).reshape(RING, piece, HD)
    sin_ref[...] = jnp.where(lane < HD // 2, -sine, sine).reshape(RING, piece, HD)

    for copy in tok_local:
        copy.wait()
    kvw_local.wait()
    both = jnp.dot(tok[0, 0], kvw[0:half_w, :], preferred_element_type=jnp.float32)
    both += jnp.dot(tok[0, 1], kvw[half_w:width, :], preferred_element_type=jnp.float32)
    kv_part[0] = both[:, 0:HD]
    kv_part[1] = both[:, HD:2 * HD]
    kv_pair = push(kv_part.at[1 - core], kv_sib, pair_out.at[0], pair_in.at[0], sibling)
    sent.append(kv_pair)

    def step(i):
        for way in range(2):
            ag_wait(i, way)
        if i + 2 <= last:
            ag_send(i + 2)

    step(0)
    kv_pair.wait_recv()
    kv_sum[...] = (kv_part[core] + kv_sib[...]).reshape(RING, piece, HD)
    kv_rows = []
    for r in range(1, RING):
        to = lax.rem(place + r, RING)
        kv_rows.append(push(
            kv_sum.at[to], kv_in.at[r], kr_out.at[r], kr_in.at[r], at(r, core)
        ))
    sent += kv_rows

    step(1)
    o_local, o_pair = [], []
    for r in range(RING):
        mine = pl.multiple_of(at(-r, core) * width, width)
        theirs = pl.multiple_of(at(-r, 1 - core) * width, width)
        o_local.append(pull(o_hbm.at[:, pl.ds(mine, width)], ow.at[r, 0:HD], o_sem.at[r]))
        o_pair.append(push(
            o_hbm.at[:, pl.ds(theirs, width)], ow.at[r, HD:2 * HD], o_out.at[r], o_in.at[r],
            sibling,
        ))
    sent += o_pair
    q_acc[...] = jnp.zeros_like(q_acc)
    for r in range(RING):
        q_local[r].wait()
        q_pair[r].wait_recv()

    for b in range(2):
        q_add(0, b)
    for i in range(2):
        for way in range(2):
            q_add(shard(way, i // 2 + 1), (i + way) % 2)

    for i in range(2, last + 1):
        step(i)
        if i == 2:
            total = kv_sum[place]
            for r in range(1, RING):
                kv_rows[r - 1].wait_recv()
                total += kv_in[r]
            turned = total * cos_ref[place] + pltpu.roll(total, HD // 2, 1) * sin_ref[place]
            is_key = (core == 0).astype(jnp.float32)
            kv_all[core, place] = (turned * is_key + total * (1.0 - is_key)).astype(jnp.bfloat16)
            kv_out = []
            for r in range(1, RING):
                kv_out.append(push(
                    kv_all.at[core, place], kv_all.at[core, place],
                    ka_out.at[r], ka_in.at[r], at(r, core),
                ))
            sent += kv_out
        if i == 5:
            for copy in kv_out:
                copy.wait_recv()
            sent.append(push(
                kv_all.at[core], kv_all.at[core], pair_out.at[3], pair_in.at[3], sibling
            ))
        for way in range(2):
            q_add(shard(way, i // 2 + 1), (i + way) % 2)

    q_send[...] = q_acc[:, HD:2 * HD]
    q_pass = push(q_send, q_recv, pair_out.at[1], pair_in.at[1], sibling)
    sent.append(q_pass)
    other_half = kv_all.at[1 - core]
    pltpu.make_async_remote_copy(
        src_ref=other_half, dst_ref=other_half, send_sem=pair_out.at[3], recv_sem=pair_in.at[3],
        device_id={"head": sibling}, device_id_type=pl.DeviceIdType.MESH,
    ).wait_recv()
    q_pass.wait_recv()
    q_raw = q_acc[:, 0:HD] + q_recv[...]
    cosine = cos_ref[...].reshape(rows, HD)
    sine = sin_ref[...].reshape(rows, HD)
    queries = (q_raw * cosine + pltpu.roll(q_raw, HD // 2, 1) * sine).astype(jnp.bfloat16)
    keys = kv_all[0].reshape(rows, HD)
    values = kv_all[1].reshape(rows, HD)
    scores = lax.dot_general(
        queries, keys, (((1,), (1,)), ((), ())), preferred_element_type=jnp.float32
    ) * (HD ** -0.5)
    scores = jnp.where(allowed, scores, -1e30)
    peak = jnp.max(scores, axis=-1, keepdims=True)
    expo = jnp.where(allowed, jnp.exp(scores - peak), 0.0)
    weights = (expo / jnp.sum(expo, axis=-1, keepdims=True)).astype(jnp.bfloat16)
    ctx[0] = jnp.dot(weights, values, preferred_element_type=jnp.float32).astype(jnp.bfloat16)
    ctx_pass = push(ctx.at[0], ctx.at[1], pair_out.at[2], pair_in.at[2], sibling)
    sent.append(ctx_pass)
    for r in range(RING):
        o_local[r].wait()
        o_pair[r].wait_recv()
    ctx_pass.wait_recv()

    context = jnp.concatenate([ctx[0], ctx[1]], axis=1)
    tile = 2 * HD

    def project(slot):
        for n in range(width // tile):
            part[slot, :, n * tile:(n + 1) * tile] = jnp.dot(
                context, ow[slot, :, n * tile:(n + 1) * tile], preferred_element_type=jnp.float32
            )

    def rs_wait(i, way):
        slot = rs_recv.at[way, i]
        pltpu.make_async_remote_copy(
            src_ref=slot, dst_ref=slot, send_sem=rs_out.at[way, i], recv_sem=rs_in.at[way, i],
            device_id={"head": ways[1 - way]}, device_id_type=pl.DeviceIdType.MESH,
        ).wait_recv()

    def rs_go(i):
        hop = (i + 1) // 2
        for way in range(2):
            slot = RING // 2 + hop if way == 0 else RING // 2 - hop
            b = (i + way) % 2
            value = part[slot, b * half_r:(b + 1) * half_r, :]
            if i >= 2:
                rs_wait(i - 2, way)
                value += rs_recv[way, i - 2].astype(jnp.float32)
            rs_send[way, i] = value.astype(jnp.bfloat16)
            sent.append(push(
                rs_send.at[way, i], rs_recv.at[way, i], rs_out.at[way, i], rs_in.at[way, i],
                ways[way],
            ))

    project(RING // 2)
    rs_go(0)
    for hop in range(1, RING // 2):
        project(RING // 2 + hop)
        project(RING // 2 - hop)
        rs_go(2 * hop - 1)
        if hop == RING // 2 - 1:
            project(0)
        rs_go(2 * hop)
    for i in (last - 1, last):
        for way in range(2):
            b = (i + way) % 2
            rs_wait(i, way)
            part[0, b * half_r:(b + 1) * half_r, :] += rs_recv[way, i].astype(jnp.float32)
    out_ref[...] = part[0].astype(out_ref.dtype)
    for copy in sent:
        copy.wait_send()


def on_ring(tokens, positions, q_weight, kv_weight, o_weight):
    rows, width = tokens.shape
    piece = rows // RING
    hops = RING - 1
    any_space = pl.BlockSpec(memory_space=pltpu.HBM)
    vmem = pl.BlockSpec(memory_space=pltpu.VMEM)
    bf16, f32 = jnp.bfloat16, jnp.float32
    dma = pltpu.SemaphoreType.DMA
    return pl.pallas_call(
        fused,
        out_shape=jax.ShapeDtypeStruct((rows, width), bf16),
        in_specs=[any_space] * 5,
        out_specs=vmem,
        scratch_shapes=[
            pltpu.VMEM((1, rows), jnp.int32),
            pltpu.VMEM((RING, piece, HD), f32),
            pltpu.VMEM((RING, piece, HD), f32),
            pltpu.VMEM((RING, 2, rows, width // 2), bf16),
            pltpu.VMEM((RING, width, 2 * HD), bf16),
            pltpu.VMEM((width, 2 * HD), bf16),
            pltpu.VMEM((RING, 2 * HD, width), bf16),
            pltpu.VMEM((rows, 2 * HD), f32),
            pltpu.VMEM((rows, HD), f32),
            pltpu.VMEM((rows, HD), f32),
            pltpu.VMEM((2, rows, HD), f32),
            pltpu.VMEM((rows, HD), f32),
            pltpu.VMEM((RING, piece, HD), f32),
            pltpu.VMEM((RING, piece, HD), f32),
            pltpu.VMEM((2, RING, piece, HD), bf16),
            pltpu.VMEM((2, rows, HD), bf16),
            pltpu.VMEM((RING, rows, width), f32),
            pltpu.VMEM((2, hops, rows // 2, width), bf16),
            pltpu.VMEM((2, hops, rows // 2, width), bf16),
            dma, dma((2,)), dma, dma((RING,)), dma((RING,)), dma((RING,)),
            dma((RING,)), dma((RING,)), dma((RING,)),
            dma((2, hops)), dma((2, hops)), dma((4,)), dma((4,)),
            dma((RING,)), dma((RING,)), dma((RING,)), dma((RING,)),
            dma((2, hops)), dma((2, hops)),
        ],
        compiler_params=pltpu.CompilerParams(
            collective_id=0, has_side_effects=True, vmem_limit_bytes=60 * 2**20
        ),
        name="prefill_ring",
    )(
        positions[None, :], tokens, q_weight.reshape(RING, CORES, width, HD), kv_weight, o_weight,
    )


def solution(mesh):
    ring = mesh.shape["head"] == RING * CORES
    return jax.shard_map(
        on_ring if ring else on_device,
        mesh=mesh,
        in_specs=(P("grp", "head"), P("grp"), P(None, "head"), P("head", None), P("head", None)),
        out_specs=P("grp", "head"),
        check_vma=False,
    )
```

```python
import math

import jax
import jax.numpy as jnp
from jax import lax
from jax.experimental import pallas as pl
from jax.experimental.pallas import tpu as pltpu
from jax.sharding import PartitionSpec as P

HD = 128
GROUP = 16


def rotate(vals, positions):
    half = vals.shape[-1] // 2
    inverse = 500000.0 ** (-(jnp.arange(half, dtype=jnp.float32) * 2.0 / vals.shape[-1]))
    angles = positions.astype(jnp.float32)[:, None] * inverse[None, :]
    cosine = jnp.cos(angles)[:, None, :]
    sine = jnp.sin(angles)[:, None, :]
    first = vals[..., :half]
    second = vals[..., half:]
    return jnp.concatenate(
        [first * cosine - second * sine, second * cosine + first * sine], axis=-1
    )


def on_device(tokens, positions, q_weight, kv_weight, o_weight):
    count_tok = tokens.shape[0]
    width = q_weight.shape[1]
    head_size = HD
    local_heads = width // head_size
    kv_width = kv_weight.shape[1]
    kv_half = kv_width // 2
    first_head = lax.axis_index("head") * local_heads
    kv_index = first_head // GROUP
    q_raw = jnp.dot(
        lax.all_gather(tokens, "head", axis=1, tiled=True),
        q_weight,
        preferred_element_type=jnp.float32,
    )
    partial_value = jnp.dot(tokens, kv_weight, preferred_element_type=jnp.float32)
    kv_raw = lax.psum(partial_value, "head")
    k_raw = lax.dynamic_slice_in_dim(kv_raw, kv_index * head_size, head_size, 1)
    v_raw = lax.dynamic_slice_in_dim(kv_raw, kv_half + kv_index * head_size, head_size, 1)
    queries = rotate(q_raw.reshape(count_tok, local_heads, head_size), positions).astype(
        jnp.bfloat16
    )
    keys = rotate(k_raw.reshape(count_tok, 1, head_size), positions)[:, 0, :].astype(jnp.bfloat16)
    values = v_raw.astype(jnp.bfloat16)
    scores = jnp.einsum(
        "qhd,kd->hqk", queries, keys, preferred_element_type=jnp.float32
    ) / jnp.sqrt(jnp.float32(head_size))
    allowed = positions[None, :] <= positions[:, None]
    scores = jnp.where(allowed[None], scores, -1e30)
    peak = jnp.max(scores, axis=-1, keepdims=True)
    expo = jnp.where(allowed[None], jnp.exp(scores - peak), 0.0)
    weights = (expo / jnp.sum(expo, axis=-1, keepdims=True)).astype(jnp.bfloat16)
    context = jnp.einsum("hqk,kd->qhd", weights, values, preferred_element_type=jnp.float32)
    context = context.astype(jnp.bfloat16).reshape(count_tok, width)
    summed = lax.psum_scatter(
        lax.dot_general(
            o_weight, context, (((0,), (1,)), ((), ())), preferred_element_type=jnp.float32
        ),
        "head",
        scatter_dimension=0,
        tiled=True,
    ).T
    return summed.astype(jnp.bfloat16)


RING = 8
CORES = 2


def head_at(place, core):
    side = lax.div(place, RING // 2)
    level = place * (1 - side) + (RING - 1 - place) * side
    return (level * 2 + side) * CORES + core


def fused(
    pos_hbm, tok_hbm, q_hbm, kv_hbm, o_hbm, out_ref, pos, cos_ref, sin_ref,
    tok, qw, kvw, ow, q_acc, q_send, q_recv, kv_part, kv_sib, kv_sum, kv_side, kv_col, kv_in, kv_all,
    ctx, part, rs_send, rs_recv,
    pos_sem, tok_sem, kvw_sem, q_sem, q_out, q_in, o_sem, o_out, o_in,
    ag_out, ag_in, pair_out, pair_in, kr_out, kr_in, ka_out, ka_in, rs_out, rs_in,
):
    rows, width = out_ref.shape
    half_w = width // 2
    half_r = rows // 2
    piece = rows // RING
    me = lax.axis_index("head")
    core = lax.rem(me, CORES)
    chip = lax.div(me, CORES)
    side = lax.rem(chip, 2)
    level = lax.div(chip, 2)
    place = level * (1 - side) + (RING - 1 - level) * side

    def at(offset, which):
        return head_at(lax.rem(place + offset + RING, RING), which)

    sibling = chip * CORES + (1 - core)
    right = at(1, core)
    left = at(-1, core)

    def push(src, dst, send, recv, target):
        copy = pltpu.make_async_remote_copy(
            src_ref=src, dst_ref=dst, send_sem=send, recv_sem=recv,
            device_id={"head": target}, device_id_type=pl.DeviceIdType.MESH,
        )
        copy.start()
        return copy

    def pull(src, dst, sem):
        copy = pltpu.make_async_copy(src, dst, sem)
        copy.start()
        return copy

    sent = []
    pos_local = pull(pos_hbm, pos, pos_sem)
    tok_local = [
        pull(tok_hbm.at[:, pl.ds(b * half_w, half_w)], tok.at[0, b], tok_sem.at[b])
        for b in range(2)
    ]
    kvw_local = pull(kv_hbm, kvw, kvw_sem)

    barrier = pltpu.get_barrier_semaphore()
    for target in [sibling] + [at(offset, core) for offset in range(1, RING)]:
        pl.semaphore_signal(
            barrier, inc=1, device_id={"head": target}, device_id_type=pl.DeviceIdType.MESH
        )
    pl.semaphore_wait(barrier, RING)

    ways = (right, left)

    def shard(way, hop):
        return hop if way == 0 else (RING - hop) % RING

    def ag_send(i):
        for way in range(2):
            b = (i + way) % 2
            hop = i // 2
            if hop == 0:
                source = tok_hbm.at[:, pl.ds(b * half_w, half_w)]
            else:
                source = tok.at[shard(way, hop), b]
            sent.append(push(
                source, tok.at[shard(way, hop + 1), b],
                ag_out.at[way, i], ag_in.at[way, i], ways[way],
            ))

    def ag_wait(i, way):
        b = (i + way) % 2
        slot = tok.at[shard(way, i // 2 + 1), b]
        pltpu.make_async_remote_copy(
            src_ref=slot, dst_ref=slot, send_sem=ag_out.at[way, i], recv_sem=ag_in.at[way, i],
            device_id={"head": ways[1 - way]}, device_id_type=pl.DeviceIdType.MESH,
        ).wait_recv()

    def q_add(slot, b):
        q_acc[...] += jnp.dot(
            tok[slot, b], qw[slot, b * half_w:(b + 1) * half_w, :],
            preferred_element_type=jnp.float32,
        )

    last = 2 * (RING // 2 - 1)
    ag_send(0)
    ag_send(1)

    q_local, q_pair = [], []
    for r in range(RING):
        owner = lax.div(at(-r, core), CORES)
        q_local.append(pull(q_hbm.at[owner, core], qw.at[r, :, 0:HD], q_sem.at[r]))
        q_pair.append(push(
            q_hbm.at[owner, 1 - core], qw.at[r, :, HD:2 * HD], q_out.at[r], q_in.at[r], sibling
        ))
    sent += q_pair

    pos_local.wait()
    pos_row = jnp.broadcast_to(pos[...].astype(jnp.float32), (rows, rows))
    pos_col = pos_row.T
    allowed = pos_row <= pos_col
    lane = lax.broadcasted_iota(jnp.int32, (rows, HD), 1)
    angle_step = lax.rem(lane, HD // 2).astype(jnp.float32) * (2.0 / HD)
    angles = pos_col * jnp.exp(angle_step * -math.log(500000.0))
    sine = jnp.sin(angles)
    cos_ref[...] = jnp.cos(angles).reshape(RING, piece, HD)
    sin_ref[...] = jnp.where(lane < HD // 2, -sine, sine).reshape(RING, piece, HD)

    for copy in tok_local:
        copy.wait()
    kvw_local.wait()
    both = jnp.dot(tok[0, 0], kvw[0:half_w, :], preferred_element_type=jnp.float32)
    both += jnp.dot(tok[0, 1], kvw[half_w:width, :], preferred_element_type=jnp.float32)
    kv_part[0] = both[:, 0:HD]
    kv_part[1] = both[:, HD:2 * HD]
    kv_pair = push(kv_part.at[1 - core], kv_sib, pair_out.at[0], pair_in.at[0], sibling)
    sent.append(kv_pair)

    def step(i):
        for way in range(2):
            ag_wait(i, way)
        if i + 2 <= last:
            ag_send(i + 2)

    step(0)
    kv_pair.wait_recv()
    kv_sum[...] = (kv_part[core] + kv_sib[...]).reshape(RING, piece, HD)
    quad = RING // 2
    across = push(
        kv_sum.at[pl.ds((1 - side) * quad, quad)], kv_side, pair_out.at[4], pair_in.at[4],
        head_at(RING - 1 - place, core),
    )
    sent.append(across)

    step(1)
    across.wait_recv()
    kv_col[...] = kv_sum[pl.ds(side * quad, quad)] + kv_side[...]
    spot = place - side * quad
    kv_rows = []
    for r in range(1, quad):
        to = lax.rem(spot + r, quad)
        kv_rows.append(push(
            kv_col.at[to], kv_in.at[r], kr_out.at[r], kr_in.at[r],
            head_at(side * quad + to, core),
        ))
    sent += kv_rows

    o_local, o_pair = [], []
    for r in range(RING):
        mine = pl.multiple_of(at(-r, core) * width, width)
        theirs = pl.multiple_of(at(-r, 1 - core) * width, width)
        o_local.append(pull(o_hbm.at[:, pl.ds(mine, width)], ow.at[r, 0:HD], o_sem.at[r]))
        o_pair.append(push(
            o_hbm.at[:, pl.ds(theirs, width)], ow.at[r, HD:2 * HD], o_out.at[r], o_in.at[r],
            sibling,
        ))
    sent += o_pair
    q_acc[...] = jnp.zeros_like(q_acc)
    for r in range(RING):
        q_local[r].wait()
        q_pair[r].wait_recv()

    for b in range(2):
        q_add(0, b)
    for i in range(2):
        for way in range(2):
            q_add(shard(way, i // 2 + 1), (i + way) % 2)

    for i in range(2, last + 1):
        step(i)
        if i == 3:
            total = kv_col[spot]
            for r in range(1, quad):
                kv_rows[r - 1].wait_recv()
                total += kv_in[r]
            turned = total * cos_ref[place] + pltpu.roll(total, HD // 2, 1) * sin_ref[place]
            is_key = (core == 0).astype(jnp.float32)
            kv_all[core, place] = (turned * is_key + total * (1.0 - is_key)).astype(jnp.bfloat16)
            kv_out = []
            for r in range(1, RING):
                kv_out.append(push(
                    kv_all.at[core, place], kv_all.at[core, place],
                    ka_out.at[r], ka_in.at[r], at(r, core),
                ))
            sent += kv_out
        if i == 5:
            for copy in kv_out:
                copy.wait_recv()
            sent.append(push(
                kv_all.at[core], kv_all.at[core], pair_out.at[3], pair_in.at[3], sibling
            ))
        for way in range(2):
            q_add(shard(way, i // 2 + 1), (i + way) % 2)

    q_send[...] = q_acc[:, HD:2 * HD]
    q_pass = push(q_send, q_recv, pair_out.at[1], pair_in.at[1], sibling)
    sent.append(q_pass)
    other_half = kv_all.at[1 - core]
    pltpu.make_async_remote_copy(
        src_ref=other_half, dst_ref=other_half, send_sem=pair_out.at[3], recv_sem=pair_in.at[3],
        device_id={"head": sibling}, device_id_type=pl.DeviceIdType.MESH,
    ).wait_recv()
    q_pass.wait_recv()
    q_raw = q_acc[:, 0:HD] + q_recv[...]
    cosine = cos_ref[...].reshape(rows, HD)
    sine = sin_ref[...].reshape(rows, HD)
    queries = (q_raw * cosine + pltpu.roll(q_raw, HD // 2, 1) * sine).astype(jnp.bfloat16)
    keys = kv_all[0].reshape(rows, HD)
    values = kv_all[1].reshape(rows, HD)
    scores = lax.dot_general(
        queries, keys, (((1,), (1,)), ((), ())), preferred_element_type=jnp.float32
    ) * (HD ** -0.5)
    scores = jnp.where(allowed, scores, -1e30)
    peak = jnp.max(scores, axis=-1, keepdims=True)
    expo = jnp.where(allowed, jnp.exp(scores - peak), 0.0)
    weights = (expo / jnp.sum(expo, axis=-1, keepdims=True)).astype(jnp.bfloat16)
    ctx[0] = jnp.dot(weights, values, preferred_element_type=jnp.float32).astype(jnp.bfloat16)
    ctx_pass = push(ctx.at[0], ctx.at[1], pair_out.at[2], pair_in.at[2], sibling)
    sent.append(ctx_pass)
    for r in range(RING):
        o_local[r].wait()
        o_pair[r].wait_recv()
    ctx_pass.wait_recv()

    context = jnp.concatenate([ctx[0], ctx[1]], axis=1)
    tile = 2 * HD

    def project(slot):
        for n in range(width // tile):
            part[slot, :, n * tile:(n + 1) * tile] = jnp.dot(
                context, ow[slot, :, n * tile:(n + 1) * tile], preferred_element_type=jnp.float32
            )

    def rs_wait(i, way):
        slot = rs_recv.at[way, i]
        pltpu.make_async_remote_copy(
            src_ref=slot, dst_ref=slot, send_sem=rs_out.at[way, i], recv_sem=rs_in.at[way, i],
            device_id={"head": ways[1 - way]}, device_id_type=pl.DeviceIdType.MESH,
        ).wait_recv()

    def rs_go(i):
        hop = (i + 1) // 2
        for way in range(2):
            slot = RING // 2 + hop if way == 0 else RING // 2 - hop
            b = (i + way) % 2
            value = part[slot, b * half_r:(b + 1) * half_r, :]
            if i >= 2:
                rs_wait(i - 2, way)
                value += rs_recv[way, i - 2].astype(jnp.float32)
            rs_send[way, i] = value.astype(jnp.bfloat16)
            sent.append(push(
                rs_send.at[way, i], rs_recv.at[way, i], rs_out.at[way, i], rs_in.at[way, i],
                ways[way],
            ))

    project(RING // 2)
    rs_go(0)
    for hop in range(1, RING // 2):
        project(RING // 2 + hop)
        project(RING // 2 - hop)
        rs_go(2 * hop - 1)
        if hop == RING // 2 - 1:
            project(0)
        rs_go(2 * hop)
    for i in (last - 1, last):
        for way in range(2):
            b = (i + way) % 2
            rs_wait(i, way)
            part[0, b * half_r:(b + 1) * half_r, :] += rs_recv[way, i].astype(jnp.float32)
    out_ref[...] = part[0].astype(out_ref.dtype)
    for copy in sent:
        copy.wait_send()


def on_ring(tokens, positions, q_weight, kv_weight, o_weight):
    rows, width = tokens.shape
    piece = rows // RING
    hops = RING - 1
    any_space = pl.BlockSpec(memory_space=pltpu.HBM)
    vmem = pl.BlockSpec(memory_space=pltpu.VMEM)
    bf16, f32 = jnp.bfloat16, jnp.float32
    dma = pltpu.SemaphoreType.DMA
    return pl.pallas_call(
        fused,
        out_shape=jax.ShapeDtypeStruct((rows, width), bf16),
        in_specs=[any_space] * 5,
        out_specs=vmem,
        scratch_shapes=[
            pltpu.VMEM((1, rows), jnp.int32),
            pltpu.VMEM((RING, piece, HD), f32),
            pltpu.VMEM((RING, piece, HD), f32),
            pltpu.VMEM((RING, 2, rows, width // 2), bf16),
            pltpu.VMEM((RING, width, 2 * HD), bf16),
            pltpu.VMEM((width, 2 * HD), bf16),
            pltpu.VMEM((RING, 2 * HD, width), bf16),
            pltpu.VMEM((rows, 2 * HD), f32),
            pltpu.VMEM((rows, HD), f32),
            pltpu.VMEM((rows, HD), f32),
            pltpu.VMEM((2, rows, HD), f32),
            pltpu.VMEM((rows, HD), f32),
            pltpu.VMEM((RING, piece, HD), f32),
            pltpu.VMEM((RING // 2, piece, HD), f32),
            pltpu.VMEM((RING // 2, piece, HD), f32),
            pltpu.VMEM((RING, piece, HD), f32),
            pltpu.VMEM((2, RING, piece, HD), bf16),
            pltpu.VMEM((2, rows, HD), bf16),
            pltpu.VMEM((RING, rows, width), f32),
            pltpu.VMEM((2, hops, rows // 2, width), bf16),
            pltpu.VMEM((2, hops, rows // 2, width), bf16),
            dma, dma((2,)), dma, dma((RING,)), dma((RING,)), dma((RING,)),
            dma((RING,)), dma((RING,)), dma((RING,)),
            dma((2, hops)), dma((2, hops)), dma((5,)), dma((5,)),
            dma((RING,)), dma((RING,)), dma((RING,)), dma((RING,)),
            dma((2, hops)), dma((2, hops)),
        ],
        compiler_params=pltpu.CompilerParams(
            collective_id=0, has_side_effects=True, vmem_limit_bytes=60 * 2**20
        ),
        name="prefill_ring",
    )(
        positions[None, :], tokens, q_weight.reshape(RING, CORES, width, HD), kv_weight, o_weight,
    )


def solution(mesh):
    ring = mesh.shape["head"] == RING * CORES
    return jax.shard_map(
        on_ring if ring else on_device,
        mesh=mesh,
        in_specs=(P("grp", "head"), P("grp"), P(None, "head"), P("head", None), P("head", None)),
        out_specs=P("grp", "head"),
        check_vma=False,
    )
```
